768 devices in a mesh: grid: 24 (over y_lo, z), band: 32 (over x, y_hi, core).
Axes of the slice: x: 4, y: 8 (y_hi: 4, y_lo: 2; y = y_hi * 2 + y_lo), z: 12, core: 2. Of those that a mesh axis runs over, the one named last changes fastest.
Arguments:
- psi_block: float32 [8, 96, 32, 128], P(None, 'grid'), may hold values from -6 to 6
- occupied: float32 [32, 96, 32, 128], P('band', 'grid'), may hold values from -6 to 6
- entry_cell: int32 [24576], P('grid'), may hold values from 0 to 16383
- entry_proj: int32 [24576], P('grid'), may hold values from 0 to 767
- entry_value: float32 [24576], P('grid'), may hold values from -3 to 3
- proj_gain: float32 [768], replicated, may hold values from 0.3 to 3
Outputs:
- applied: float32 [8, 96, 32, 128], P(None, 'grid')
The draws below stay inside these ranges and needn't reach their ends.
All inputs are finite; a program needn't handle non-finite values.
Results may differ from the reference program's by a relative error of at most 0.00002.
Values sent between devices are 32-bit elements; how exact they have to be, the bound alone decides.
A program may use at most 64 MiB of HBM per device.

```python
import math
import jax
import jax.numpy as jnp
import numpy as np
from jax import lax

BLOCK = 8
PX = 4
NY = 32
NZ = 128
SWEEPS = 4
ENT_DEV = 1024
NX = 96
OCC = 32
PROJS = 768
ENTRIES = 24576


def with_ends(array, own_key, least, high):
    spot = [jax.random.randint(jax.random.fold_in(own_key, axis), (), 0, length) for axis, length in enumerate(array.shape)]
    main_axis = array.shape.index(max(array.shape))
    beside = spot[:main_axis] + [(spot[main_axis] + 1) % array.shape[main_axis]] + spot[main_axis + 1:]
    return array.at[tuple(spot)].set(least).at[tuple(beside)].set(high)


def shard_levels(rng, dims, cuts, least, high):
    def one(axis_at, parts):
        steps = jax.random.uniform(jax.random.fold_in(jax.random.fold_in(rng, 6), axis_at), (parts,), jnp.float32, least / len(cuts), high / len(cuts))
        return jnp.repeat(jnp.exp(steps), dims[axis_at] // parts).reshape((-1,) + (1,) * (len(dims) - axis_at - 1))

    level = one(*cuts[0])
    for cut in cuts[1:]:
        level = level * one(*cut)
    return level


def rank_bounds(amount, skew):
    loads = [(1 << 20) // math.isqrt(standing ** skew) + 1 for standing in range(1, amount + 1)]
    width = 1 + sum(loads) // (1 << 30)
    return np.cumsum(np.array([max(1, weight // width) for weight in loads]))


def ranked_ids(own_key, extent, number_of, skew):
    listing = rank_bounds(number_of, skew)
    lot = jax.random.randint(jax.random.fold_in(own_key, 1), extent, 0, int(listing[number_of - 1]))
    grade = jnp.searchsorted(jnp.asarray(listing, jnp.int32), lot, side="right")
    return jax.random.permutation(jax.random.fold_in(own_key, 2), number_of)[grade].astype(jnp.int32)


def noise(stream_key, shape, scale, bound, split=(), held_as=jnp.bfloat16):
    drawn = jax.random.normal(stream_key, shape, jnp.float32) * scale
    if len(split) > 0:
        drawn = shard_levels(stream_key, shape, split, -0.22, 0.18) * drawn
    return jnp.clip(drawn, min=-bound, max=bound).astype(held_as)


def setup_inputs(seed: int = 0) -> dict:
    key_of = jax.random.split(jax.random.key(seed), 7)
    psi_block = noise(key_of[0], (BLOCK, NX, NY, NZ), 1.0, 6.0, ((1, 24),), jnp.float32)
    occupied = noise(key_of[1], (OCC, NX, NY, NZ), 1.0, 6.0, ((0, 32), (1, 24)), jnp.float32)
    entry_cell = with_ends(jax.random.randint(key_of[2], (ENTRIES,), 0, PX * NY * NZ), jax.random.fold_in(key_of[2], 1), 0, (PX * NY * NZ) - 1).astype(jnp.int32)
    entry_proj = with_ends(ranked_ids(key_of[3], (ENTRIES,), PROJS, 1), jax.random.fold_in(key_of[3], 3), 0, PROJS - 1).astype(jnp.int32)
    entry_value = noise(key_of[4], (ENTRIES,), 0.5, 3.0, ((0, 24),), jnp.float32)
    proj_gain = jnp.clip(jnp.exp(jax.random.uniform(key_of[5], (PROJS,), jnp.float32, math.log(0.3), math.log(3.0))), 0.3, 3.0)
    return dict(psi_block=psi_block, occupied=occupied, entry_cell=entry_cell, entry_proj=entry_proj, entry_value=entry_value, proj_gain=proj_gain)


screening = 0.5
mixing = 0.25


def neighbours(field):
    summed = jnp.roll(field, -1, 1) + jnp.roll(field, 1, 1)
    summed = summed + jnp.roll(field, -1, 2) + jnp.roll(field, 1, 2)
    summed = summed + jnp.roll(field, -1, 3) + jnp.roll(field, 1, 3)
    return summed


def reference(psi_block, occupied, entry_cell, entry_proj, entry_value, proj_gain):
    slab_cells = PX * NY * NZ
    flattened = psi_block.reshape(BLOCK, NX * NY * NZ)
    owners = (jnp.arange(ENTRIES, dtype=jnp.int32) // ENT_DEV).astype(jnp.int32)
    global_cell = owners * slab_cells + entry_cell
    values = flattened[:, global_cell]
    coefficient = jax.ops.segment_sum((values * entry_value[None, :]).T, entry_proj, num_segments=PROJS)
    scaled = coefficient * proj_gain[:, None]
    contrib = entry_value[:, None] * scaled[entry_proj]
    nonlocal_term = jax.ops.segment_sum(contrib, global_cell, num_segments=NX * NY * NZ).T.reshape(psi_block.shape)
    kinetic = -0.5 * (neighbours(psi_block) - 6.0 * psi_block)

    def accumulate(summed, orbital):
        density = psi_block * orbital[None]
        potential = density / (6.0 + screening)
        for repeat_index in range(SWEEPS - 1):
            potential = (neighbours(potential) + density) / (6.0 + screening)
        return summed + orbital[None] * potential, None

    summed, unused = lax.scan(accumulate, jnp.zeros(psi_block.shape, jnp.float32), occupied)
    exchange = -mixing * summed
    return kinetic + nonlocal_term + exchange
```

```python
import functools

import jax
import jax.numpy as jnp
from jax import lax
from jax.experimental import pallas as pl
from jax.experimental.pallas import tpu as pltpu
from jax.sharding import PartitionSpec as P

screening = 0.5
mixing = 0.25
WIDTH = 3
LANES = 128
CORES = 2
XS, YS = 4, 4
RADIX = ((1, 4), (4, 3), (12, 2))
GROUPS = 4
MESH = pl.DeviceIdType.MESH


def three_parts(x):
    first = x.astype(jnp.bfloat16)
    rest = x - first.astype(jnp.float32)
    second = rest.astype(jnp.bfloat16)
    third = (rest - second.astype(jnp.float32)).astype(jnp.bfloat16)
    return jnp.concatenate([first, second, third], axis=0)


def add_parts(x):
    n = x.shape[0] // 3
    return (x[:n] + x[n : 2 * n]) + x[2 * n :]


def as_row(x):
    return jnp.concatenate([x[i : i + 1] for i in range(x.shape[0])], axis=1)


def roll_sum(u):
    rows, lanes = u.shape[-2:]
    a = u.ndim - 2
    return (pltpu.roll(u, 1, a) + pltpu.roll(u, rows - 1, a)) + (
        pltpu.roll(u, 1, a + 1) + pltpu.roll(u, lanes - 1, a + 1)
    )


def kernel(
    nocc_cores,
    psi, occ, cell, proj, value, gain,
    out,
    psi_ext, occ_ext, cell_v, proj_v, value_v, gain_v,
    hot_lane, hot_proj, part, rs1, red1, rs2, kin, csum, cin, call_, out_v,
    local_sem, send_sem, recv_sem,
):
    planes, rows = psi.shape[1], psi.shape[2]
    orbs = psi.shape[0] // CORES
    per = orbs // GROUPS
    ppx, rpy = planes // XS, rows // YS
    entries = cell.shape[0] * cell.shape[1]
    size = lax.axis_size("grid")
    g, n = lax.axis_index("grid"), lax.axis_index("band")
    c = n % CORES
    y = (n // CORES) % YS
    x = n // (CORES * YS)

    def band(xx, yy, cc):
        return (xx * YS + yy) * CORES + cc

    nxt, prv = (g + 1) % size, (g + size - 1) % size
    sibling = (g, band(x, y, 1 - c))
    xpeers = [(g, band((x + m) % XS, y, c)) for m in range(1, XS)]
    ypeers = [(g, band(x, (y + m) % YS, c)) for m in range(1, YS)]
    gpeers = []
    for stride, count in RADIX:
        digit = (g // stride) % count
        gpeers.append([(g + ((digit + m) % count - digit) * stride, n) for m in range(1, count)])

    def local(i, src, dst):
        copy = pltpu.make_async_copy(src, dst, local_sem.at[i])
        copy.start()
        return copy

    first = c * orbs
    load_entries = [
        local(0, cell, cell_v), local(1, proj, proj_v), local(2, value, value_v), local(3, gain, gain_v),
    ]
    load_psi = local(4, psi.at[pl.ds(first, orbs)], psi_ext.at[:, pl.ds(WIDTH, planes)])
    load_occ = local(5, occ.at[0], occ_ext.at[c, pl.ds(WIDTH, planes)])

    partners = [(nxt, n), (prv, n), sibling] + xpeers + ypeers + [d for ds in gpeers for d in ds]
    barrier = pltpu.get_barrier_semaphore()
    for device in partners:
        pl.semaphore_signal(barrier, inc=1, device_id=device, device_id_type=MESH)
    pl.semaphore_wait(barrier, len(partners))

    copies = []

    def send(src, dst, device):
        i = len(copies)
        copy = pltpu.make_async_remote_copy(
            src_ref=src, dst_ref=dst, send_sem=send_sem.at[i], recv_sem=recv_sem.at[i],
            device_id=device, device_id_type=MESH,
        )
        copy.start()
        copies.append(copy)
        return copy

    low, high = pl.ds(0, WIDTH), pl.ds(WIDTH + planes, WIDTH)
    upper, lower = pl.ds(planes - WIDTH, WIDTH), pl.ds(0, WIDTH)
    occ_up = send(occ.at[0, upper], occ_ext.at[c, low], (nxt, n))
    occ_down = send(occ.at[0, lower], occ_ext.at[c, high], (prv, n))
    occ_core = send(occ.at[0], occ_ext.at[c, pl.ds(WIDTH, planes)], sibling)
    halos = []
    for k in range(GROUPS):
        mine, there = pl.ds(first + k * per, per), pl.ds(k * per, per)
        halos.append([
            send(psi.at[mine, upper], psi_ext.at[there, low], (nxt, n)),
            send(psi.at[mine, lower], psi_ext.at[there, high], (prv, n)),
        ])

    for copy in load_entries:
        copy.wait()
    cells, projs, values = as_row(cell_v[...]), as_row(proj_v[...]), as_row(value_v[...])
    cell_row, cell_lane = cells // LANES, cells % LANES
    proj_row, proj_lane = projs // LANES, projs % LANES
    lanes_at = lax.broadcasted_iota(jnp.int32, (LANES, entries), 0)
    hot_lane[...] = jnp.where(lanes_at == cell_lane, 1.0, 0.0).astype(jnp.bfloat16)
    hot_proj[...] = jnp.where(lanes_at == proj_lane, 1.0, 0.0).astype(jnp.bfloat16)
    eight = lax.broadcasted_iota(jnp.int32, (8, entries), 0)
    proj_mask = eight == proj_row

    load_psi.wait()
    load_occ.wait()
    nn = (((1,), (0,)), ((), ()))
    nt = (((1,), (1,)), ((), ()))

    def dot(a, b, dims):
        return lax.dot_general(a, b, dims, preferred_element_type=jnp.float32)

    cut = orbs // XS if orbs >= XS else 1
    for q in range(cut):
        own = psi_ext[x * cut + q, pl.ds(WIDTH, planes)].reshape(planes * rows, LANES)
        spread = add_parts(dot(three_parts(own), hot_lane[...], nn))
        at = lax.broadcasted_iota(jnp.int32, (planes * rows, entries), 0)
        picked = jnp.sum(jnp.where(at == cell_row, spread, 0.0), axis=0, keepdims=True)
        weight = jnp.where(proj_mask, picked * values, 0.0)
        csum[0, q] = add_parts(dot(three_parts(weight), hot_proj[...], nt))

    def coefficients(stage):
        base = sum(count - 1 for _, count in RADIX[:stage])
        return [send(csum.at[stage], cin.at[base + m], device) for m, device in enumerate(gpeers[stage])]

    def collect(stage, sent):
        base = sum(count - 1 for _, count in RADIX[:stage])
        total = csum[stage]
        for m, copy in enumerate(sent):
            copy.wait_recv()
            total = total + cin[base + m]
        csum[stage + 1] = total

    in_flight = coefficients(0)

    occ_up.wait_recv()
    forward_up = send(occ_ext.at[c, low], occ_ext.at[c, low], sibling)
    occ_down.wait_recv()
    forward_down = send(occ_ext.at[c, high], occ_ext.at[c, high], sibling)

    inverse = 1.0 / (6.0 + screening)

    def exchange(k):
        def one(j, total):
            orbital = occ_ext[j]
            density = psi_ext[k] * orbital
            u = density * inverse
            for s in range(1, WIDTH + 1):
                d = density[s : density.shape[0] - s]
                u = ((u[2:] + u[:-2]) + (roll_sum(u[1:-1]) + d)) * inverse
            return total + orbital[WIDTH : WIDTH + planes] * u

        part[k] = lax.fori_loop(0, CORES, one, jnp.zeros(part.shape[1:], jnp.float32))

    def scatter_x(k):
        sent = []
        for m, device in enumerate(xpeers):
            there = pl.ds(((x + m + 1) % XS) * ppx, ppx)
            sent.append(send(part.at[pl.ds(k * per, per), there], rs1.at[pl.ds(k * per, per), m], device))
        return sent

    def scatter_y(k, sent):
        total = part[pl.ds(k * per, per), pl.ds(x * ppx, ppx)]
        for m, copy in enumerate(sent):
            copy.wait_recv()
            total = total + rs1[pl.ds(k * per, per), m]
        red1[pl.ds(k * per, per)] = total
        later = []
        for m, device in enumerate(ypeers):
            there = pl.ds(pl.multiple_of(((y + m + 1) % YS) * rpy, rpy), rpy)
            later.append(send(red1.at[pl.ds(k * per, per), :, there], rs2.at[pl.ds(k * per, per), m], device))
        return later

    own_rows = pl.ds(pl.multiple_of(y * rpy, rpy), rpy)
    first_sent, second_sent = {}, {}
    for k in range(GROUPS + 1):
        if k < GROUPS:
            for copy in halos[k]:
                copy.wait_recv()
            if k == 0:
                occ_core.wait_recv()
                forward_up.wait_recv()
                forward_down.wait_recv()
            for i in range(k * per, (k + 1) * per):
                exchange(i)
            first_sent[k] = scatter_x(k)
            if k < len(RADIX):
                collect(k, in_flight)
                if k + 1 < len(RADIX):
                    in_flight = coefficients(k + 1)
        if k > 0:
            second_sent[k - 1] = scatter_y(k - 1, first_sent[k - 1])
    for k in range(GROUPS, len(RADIX)):
        collect(k, in_flight)
        if k + 1 < len(RADIX):
            in_flight = coefficients(k + 1)

    gains = jnp.concatenate([gain_v[...], jnp.zeros((8 - gain_v.shape[0], LANES), jnp.float32)], axis=0)
    for q in range(cut):
        call_[x * cut + q] = csum[len(RADIX), q] * gains
    mine = pl.ds(x * cut, cut)
    in_flight = [send(call_.at[mine], call_.at[mine], device) for device in xpeers]

    for k in range(orbs):
        for q in range(ppx):
            at = WIDTH + x * ppx + q
            centre = psi_ext[k, at]
            around = (psi_ext[k, at + 1] + psi_ext[k, at - 1]) + roll_sum(centre)
            kin[k, q] = -0.5 * (around - 6.0 * centre)

    for copy in in_flight:
        copy.wait_recv()
    found = add_parts(dot(three_parts(call_[...].reshape(orbs * 8, LANES)), hot_proj[...], nn))
    target = []
    for k in range(orbs):
        picked = jnp.sum(jnp.where(proj_mask, found[k * 8 : (k + 1) * 8], 0.0), axis=0, keepdims=True)
        target.append(picked * values)
    at = lax.broadcasted_iota(jnp.int32, (rpy, entries), 0)
    nonlocal_terms = []
    for q in range(ppx):
        row_mask = at + ((x * ppx + q) * rows + y * rpy) == cell_row
        spread = jnp.concatenate([jnp.where(row_mask, t, 0.0) for t in target], axis=0)
        nonlocal_terms.append(add_parts(dot(three_parts(spread), hot_lane[...], nt)).reshape(orbs, 1, rpy, LANES))
    nonlocal_term = jnp.concatenate(nonlocal_terms, axis=1)

    total = red1[:, :, own_rows]
    for k in range(GROUPS):
        for copy in second_sent[k]:
            copy.wait_recv()
    for m in range(YS - 1):
        total = total + rs2[:, m]
    own_orbs, own_planes = pl.ds(first, orbs), pl.ds(x * ppx, ppx)
    out_v[own_orbs, own_planes, own_rows] = (kin[:, :, own_rows] + nonlocal_term) - mixing * total

    block = out_v.at[own_orbs, own_planes, own_rows]
    in_flight = [send(block, block, device) for device in ypeers]
    for copy in in_flight:
        copy.wait_recv()
    block = out_v.at[own_orbs, own_planes]
    in_flight = [send(block, block, device) for device in xpeers]
    to_core = [send(block, out.at[own_orbs, own_planes], sibling)]
    stores = [local(6, block, out.at[own_orbs, own_planes])]
    for m, copy in enumerate(in_flight):
        copy.wait_recv()
        at = pl.ds(((x + XS - 1 - m) % XS) * ppx, ppx)
        block = out_v.at[own_orbs, at]
        to_core.append(send(block, out.at[own_orbs, at], sibling))
        stores.append(local(7 + m, block, out.at[own_orbs, at]))
    for copy in to_core:
        copy.wait_recv()
    for copy in stores:
        copy.wait()
    for copy in copies:
        copy.wait_send()


def n_copies():
    coefficient = sum(count - 1 for _, count in RADIX) + XS - 1
    return 3 + 2 + GROUPS * (2 + XS - 1 + YS - 1) + coefficient + (YS - 1) + (XS - 1) + XS


def per_device(psi_block, occupied, entry_cell, entry_proj, entry_value, proj_gain):
    nblock, planes, rows, lanes = psi_block.shape
    orbs = nblock // CORES
    entries = entry_cell.shape[0]
    f32 = jnp.float32
    table = (entries // LANES, LANES)
    ext = planes + 2 * WIDTH
    ppx, rpy = planes // XS, rows // YS
    cut = orbs // XS if orbs >= XS else 1
    gains = proj_gain.reshape(-1, LANES)
    total = n_copies()
    any_ = pl.BlockSpec(memory_space=pl.ANY)
    return pl.pallas_call(
        functools.partial(kernel, CORES),
        out_shape=jax.ShapeDtypeStruct(psi_block.shape, f32),
        in_specs=[pl.BlockSpec(memory_space=pltpu.HBM)] * 6,
        out_specs=any_,
        scratch_shapes=[
            pltpu.VMEM((orbs, ext, rows, lanes), f32),
            pltpu.VMEM((CORES, ext, rows, lanes), f32),
            pltpu.VMEM(table, jnp.int32),
            pltpu.VMEM(table, jnp.int32),
            pltpu.VMEM(table, f32),
            pltpu.VMEM(gains.shape, f32),
            pltpu.VMEM((LANES, entries), jnp.bfloat16),
            pltpu.VMEM((LANES, entries), jnp.bfloat16),
            pltpu.VMEM((orbs, planes, rows, lanes), f32),
            pltpu.VMEM((orbs, XS - 1, ppx, rows, lanes), f32),
            pltpu.VMEM((orbs, ppx, rows, lanes), f32),
            pltpu.VMEM((orbs, YS - 1, ppx, rpy, lanes), f32),
            pltpu.VMEM((orbs, ppx, rows, lanes), f32),
            pltpu.VMEM((len(RADIX) + 1, cut, 8, lanes), f32),
            pltpu.VMEM((sum(count - 1 for _, count in RADIX), cut, 8, lanes), f32),
            pltpu.VMEM((orbs, 8, lanes), f32),
            pltpu.VMEM(psi_block.shape, f32),
            pltpu.SemaphoreType.DMA((7 + XS - 1,)),
            pltpu.SemaphoreType.DMA((total,)),
            pltpu.SemaphoreType.DMA((total,)),
        ],
        compiler_params=pltpu.CompilerParams(
            collective_id=0, has_side_effects=True, vmem_limit_bytes=60 * 1024 * 1024
        ),
        cost_estimate=pl.CostEstimate(flops=20_000_000, bytes_accessed=2_000_000, transcendentals=0),
    )(
        psi_block, occupied, entry_cell.reshape(table), entry_proj.reshape(table),
        entry_value.reshape(table), gains,
    )


def solution(mesh):
    in_specs = (
        P(None, "grid", None, None),
        P("band", "grid", None, None),
        P("grid"),
        P("grid"),
        P("grid"),
        P(),
    )
    out_specs = P(None, "grid", None, None)
    return jax.shard_map(
        per_device, mesh=mesh, in_specs=in_specs, out_specs=out_specs, check_vma=False
    )
```

```python
import functools

import jax
import jax.numpy as jnp
from jax import lax
from jax.experimental import pallas as pl
from jax.experimental.pallas import tpu as pltpu
from jax.sharding import PartitionSpec as P

screening = 0.5
mixing = 0.25
WIDTH = 3
LANES = 128
CORES = 2
XS, YS = 4, 4
STEPS = ((1, 2), (2, 2), (0, 2), (4, 3))
YLO = 2
DIRECT = 1
GROUPS = 4
FIRST = 2
MESH = pl.DeviceIdType.MESH


def three_parts(x):
    first = x.astype(jnp.bfloat16)
    rest = x - first.astype(jnp.float32)
    second = rest.astype(jnp.bfloat16)
    third = (rest - second.astype(jnp.float32)).astype(jnp.bfloat16)
    return jnp.concatenate([first, second, third], axis=0)


def add_parts(x):
    n = x.shape[0] // 3
    return (x[:n] + x[n : 2 * n]) + x[2 * n :]


def as_row(x):
    return jnp.concatenate([x[i : i + 1] for i in range(x.shape[0])], axis=1)


def roll_sum(u):
    rows, lanes = u.shape[-2:]
    a = u.ndim - 2
    return (pltpu.roll(u, 1, a) + pltpu.roll(u, rows - 1, a)) + (
        pltpu.roll(u, 1, a + 1) + pltpu.roll(u, lanes - 1, a + 1)
    )


def kernel(
    nocc_cores,
    psi, occ, cell, proj, value, gain,
    out,
    psi_ext, occ_ext, cell_v, proj_v, value_v, gain_v,
    hot_lane, hot_proj, part, rs1, red1, rs2, kin, csum, cin, call_,
    local_sem, send_sem, recv_sem, step_sem,
):
    planes, rows = psi.shape[1], psi.shape[2]
    orbs = psi.shape[0] // CORES
    per = orbs // GROUPS
    ppx = planes // XS
    entries = cell.shape[0] * cell.shape[1]
    size = lax.axis_size("grid")
    ring = size // YLO
    g, n = lax.axis_index("grid"), lax.axis_index("band")
    c = lax.rem(n, CORES)
    y = lax.rem(lax.div(n, CORES), YS)
    x = lax.div(n, CORES * YS)

    def wrap(i, length):
        return jnp.where(i >= length, i - length, i)

    def band(xx, yy, cc):
        return (xx * YS + yy) * CORES + cc

    nxt, prv = (wrap(g + 1, size), n), (wrap(g + size - 1, size), n)
    sibling = (g, band(x, y, 1 - c))
    xpeers = [(g, band(wrap(x + m, XS), y, c)) for m in range(1, XS)]
    ypeers = [(g, band(x, wrap(y + m, YS), c)) for m in range(1, YS)]
    z = g
    for i in range(1, YLO):
        z = jnp.where(g >= i * ring, g - i * ring, z)
    turn = g - z

    def along(m):
        return (turn + wrap(z + m % ring, ring), n)

    across = [(wrap(g + m * ring, size), n) for m in range(1, YLO)]

    partners = [nxt, prv, sibling, along(1), along(-1)] + across
    partners += [peers[i] for peers in (xpeers, ypeers) if peers for i in (0, -1)]
    barrier = pltpu.get_barrier_semaphore()

    def signal(semaphore, device):
        pl.semaphore_signal(semaphore, inc=1, device_id=device, device_id_type=MESH)

    for device in partners:
        signal(barrier, device)

    def local(i, src, dst):
        copy = pltpu.make_async_copy(src, dst, local_sem.at[i])
        copy.start()
        return copy

    first = c * orbs
    load_entries = [
        local(0, cell, cell_v), local(1, proj, proj_v), local(2, value, value_v), local(3, gain, gain_v),
    ]
    load_psi = local(4, psi.at[pl.ds(first, orbs)], psi_ext.at[:, pl.ds(WIDTH, planes)])
    load_occ = local(5, occ.at[0], occ_ext.at[c, pl.ds(WIDTH, planes)])

    for copy in load_entries:
        copy.wait()
    cells, projs, values = as_row(cell_v[...]), as_row(proj_v[...]), as_row(value_v[...])
    cell_row, cell_lane = cells // LANES, cells % LANES
    proj_row, proj_lane = projs // LANES, projs % LANES
    lanes_at = lax.broadcasted_iota(jnp.int32, (LANES, entries), 0)
    hot_lane[...] = jnp.where(lanes_at == cell_lane, 1.0, 0.0).astype(jnp.bfloat16)
    hot_proj[...] = jnp.where(lanes_at == proj_lane, 1.0, 0.0).astype(jnp.bfloat16)
    eight = lax.broadcasted_iota(jnp.int32, (8, entries), 0)
    proj_mask = eight == proj_row

    load_psi.wait()
    load_occ.wait()
    nn = (((1,), (0,)), ((), ()))
    nt = (((1,), (1,)), ((), ()))

    def dot(a, b, dims):
        return lax.dot_general(a, b, dims, preferred_element_type=jnp.float32)

    cut = orbs // XS if orbs >= XS else 1
    for q in range(cut):
        own = psi_ext[x * cut + q, pl.ds(WIDTH, planes)].reshape(planes * rows, LANES)
        spread = add_parts(dot(three_parts(own), hot_lane[...], nn))
        at = lax.broadcasted_iota(jnp.int32, (planes * rows, entries), 0)
        picked = jnp.sum(jnp.where(at == cell_row, spread, 0.0), axis=0, keepdims=True)
        weight = jnp.where(proj_mask, picked * values, 0.0)
        csum[0, q] = add_parts(dot(three_parts(weight), hot_proj[...], nt))

    pl.semaphore_wait(barrier, len(partners))

    copies = []

    def send(src, dst, device):
        i = len(copies)
        copy = pltpu.make_async_remote_copy(
            src_ref=src, dst_ref=dst, send_sem=send_sem.at[i], recv_sem=recv_sem.at[i],
            device_id=device, device_id_type=MESH,
        )
        copy.start()
        copies.append(copy)
        return copy

    low, high = pl.ds(0, WIDTH), pl.ds(WIDTH + planes, WIDTH)
    upper, lower = pl.ds(planes, WIDTH), pl.ds(WIDTH, WIDTH)

    def halo(k):
        there = pl.ds(k * per, per)
        return [
            send(psi_ext.at[there, upper], psi_ext.at[there, low], nxt),
            send(psi_ext.at[there, lower], psi_ext.at[there, high], prv),
        ]

    word = [i for i, (distance, terms) in enumerate(STEPS[:-1]) if distance and terms == 2]

    def coefficients(stage):
        base = sum(terms - 1 for _, terms in STEPS[:stage])
        distance, terms = STEPS[stage]
        if not distance:
            devices = across
        elif terms == 2:
            devices = [along(-distance)]
            if stage in word:
                signal(step_sem.at[1 + stage], along(distance))
        else:
            devices = [along(distance), along(-distance)]
        return [send(csum.at[stage], cin.at[base + m], device) for m, device in enumerate(devices)]

    def collect(stage, sent):
        base = sum(terms - 1 for _, terms in STEPS[:stage])
        total = csum[stage]
        for m, copy in enumerate(sent):
            copy.wait_recv()
            total = total + cin[base + m]
        csum[stage + 1] = total
        if stage in word:
            pl.semaphore_wait(step_sem.at[1 + stage], 1)

    stages = len(STEPS)
    steps = [coefficients(0)]

    def next_step():
        stage = len(steps) - 1
        if stage >= stages:
            return
        collect(stage, steps[stage])
        steps.append(coefficients(stage + 1) if stage + 1 < stages else None)

    occ_halo = [
        send(occ_ext.at[c, upper], occ_ext.at[c, low], nxt), send(occ_ext.at[c, lower], occ_ext.at[c, high], prv),
    ]
    centre = occ_ext.at[c, pl.ds(WIDTH, planes)]
    occ_core = send(centre, centre, sibling)
    halos = [halo(k) for k in range(FIRST)]
    greeted = [peers[-1] for peers in (xpeers, ypeers) if peers]
    for device in greeted:
        signal(step_sem.at[0], device)
    next_step()
    halos += [halo(k) for k in range(FIRST, GROUPS)]
    for copy, part_ in zip(occ_halo, (low, high)):
        copy.wait_recv()
        block = occ_ext.at[c, part_]
        send(block, block, sibling)
    forwards = copies[-2:]

    inverse = 1.0 / (6.0 + screening)

    def exchange(k):
        def one(j, total):
            orbital = occ_ext[j]
            density = psi_ext[k] * orbital
            u = density * inverse
            for s in range(1, WIDTH + 1):
                d = density[s : density.shape[0] - s]
                u = ((u[2:] + u[:-2]) + (roll_sum(u[1:-1]) + d)) * inverse
            return total + orbital[WIDTH : WIDTH + planes] * u

        part[k] = lax.fori_loop(0, CORES, one, jnp.zeros(part.shape[1:], jnp.float32))

    def scatter_x(k):
        sent = []
        for m, device in enumerate(xpeers):
            there = pl.ds(((x + m + 1) % XS) * ppx, ppx)
            sent.append(send(part.at[pl.ds(k * per, per), there], rs1.at[pl.ds(k * per, per), m], device))
        return sent

    def sum_x(k, sent):
        own = pl.ds(k * per, per)
        total = part[own, pl.ds(x * ppx, ppx)]
        for m, copy in enumerate(sent):
            copy.wait_recv()
            total = total + rs1[own, m]
        red1[own] = total
        return [send(red1.at[own], rs2.at[own, m], device) for m, device in enumerate(ypeers)]

    def share_coefficients():
        while len(steps) <= stages:
            next_step()
        gains = jnp.concatenate([gain_v[...], jnp.zeros((8 - gain_v.shape[0], LANES), jnp.float32)], axis=0)
        for q in range(cut):
            call_[x * cut + q] = csum[stages, q] * gains
        mine = pl.ds(x * cut, cut)
        return [send(call_.at[mine], call_.at[mine], device) for device in xpeers]

    first_sent, second_sent = [], []
    for k in range(GROUPS):
        for copy in halos[k]:
            copy.wait_recv()
        if k == 0:
            for copy in [occ_core] + forwards:
                copy.wait_recv()
            pl.semaphore_wait(step_sem.at[0], len(greeted))
        for i in range(k * per, (k + 1) * per):
            exchange(i)
        first_sent.append(scatter_x(k))
        if k == 1:
            next_step()
    next_step()
    for k in range(GROUPS):
        second_sent.append(sum_x(k, first_sent[k]))
    share = share_coefficients()

    for k in range(orbs):
        for q in range(ppx):
            at = WIDTH + x * ppx + q
            centre = psi_ext[k, at]
            around = (psi_ext[k, at + 1] + psi_ext[k, at - 1]) + roll_sum(centre)
            kin[k, q] = -0.5 * (around - 6.0 * centre)

    for copy in share:
        copy.wait_recv()
    found = add_parts(dot(three_parts(call_[...].reshape(orbs * 8, LANES)), hot_proj[...], nn))
    target = []
    for k in range(orbs):
        picked = jnp.sum(jnp.where(proj_mask, found[k * 8 : (k + 1) * 8], 0.0), axis=0, keepdims=True)
        target.append(picked * values)
    at = lax.broadcasted_iota(jnp.int32, (rows, entries), 0)
    for q in range(ppx):
        row_mask = at + (x * ppx + q) * rows == cell_row
        spread = jnp.concatenate([jnp.where(row_mask, t, 0.0) for t in target], axis=0)
        found = add_parts(dot(three_parts(spread), hot_lane[...], nt))
        for k in range(orbs):
            kin[k, q] = kin[k, q] + found[k * rows : (k + 1) * rows]

    xcross = [(g, band(wrap(x + m, XS), y, 1 - c)) for m in range(1, XS)]
    gathered = []
    for k in range(GROUPS):
        own = pl.ds(k * per, per)
        total = red1[own]
        for m, copy in enumerate(second_sent[k]):
            copy.wait_recv()
            total = total + rs2[own, m]
        there = pl.ds(first + k * per, per)
        block = out.at[there, pl.ds(x * ppx, ppx)]
        out[there, pl.ds(x * ppx, ppx)] = kin[own] - mixing * total
        last = k >= GROUPS - DIRECT
        gathered.append([send(block, block, device) for device in xpeers + (xcross if last else []) + [sibling]])
    for k in range(GROUPS - DIRECT):
        for m, copy in enumerate(gathered[k][:-1]):
            copy.wait_recv()
            there = pl.ds(wrap(x + XS - 1 - m, XS) * ppx, ppx)
            block = out.at[pl.ds(first + k * per, per), there]
            gathered[k].append(send(block, block, sibling))
        gathered[k] = gathered[k][XS - 1 :]
    for sent in gathered:
        for copy in sent:
            copy.wait_recv()
    for copy in copies:
        copy.wait_send()


def n_copies():
    coefficient = sum(terms - 1 for _, terms in STEPS) + XS - 1
    return 3 + 2 + GROUPS * (2 + (XS - 1) + (YS - 1) + 2 * XS - 1) + coefficient


def per_device(psi_block, occupied, entry_cell, entry_proj, entry_value, proj_gain):
    nblock, planes, rows, lanes = psi_block.shape
    orbs = nblock // CORES
    entries = entry_cell.shape[0]
    f32 = jnp.float32
    table = (entries // LANES, LANES)
    ext = planes + 2 * WIDTH
    ppx = planes // XS
    cut = orbs // XS if orbs >= XS else 1
    gains = proj_gain.reshape(-1, LANES)
    total = n_copies()
    return pl.pallas_call(
        functools.partial(kernel, CORES),
        out_shape=pltpu.VMEM(psi_block.shape, f32),
        in_specs=[pl.BlockSpec(memory_space=pltpu.HBM)] * 6,
        out_specs=pl.BlockSpec(memory_space=pltpu.VMEM),
        scratch_shapes=[
            pltpu.VMEM((orbs, ext, rows, lanes), f32),
            pltpu.VMEM((CORES, ext, rows, lanes), f32),
            pltpu.VMEM(table, jnp.int32),
            pltpu.VMEM(table, jnp.int32),
            pltpu.VMEM(table, f32),
            pltpu.VMEM(gains.shape, f32),
            pltpu.VMEM((LANES, entries), jnp.bfloat16),
            pltpu.VMEM((LANES, entries), jnp.bfloat16),
            pltpu.VMEM((orbs, planes, rows, lanes), f32),
            pltpu.VMEM((orbs, XS - 1, ppx, rows, lanes), f32),
            pltpu.VMEM((orbs, ppx, rows, lanes), f32),
            pltpu.VMEM((orbs, YS - 1, ppx, rows, lanes), f32),
            pltpu.VMEM((orbs, ppx, rows, lanes), f32),
            pltpu.VMEM((len(STEPS) + 1, cut, 8, lanes), f32),
            pltpu.VMEM((sum(terms - 1 for _, terms in STEPS), cut, 8, lanes), f32),
            pltpu.VMEM((orbs, 8, lanes), f32),
            pltpu.SemaphoreType.DMA((6,)),
            pltpu.SemaphoreType.DMA((total,)),
            pltpu.SemaphoreType.DMA((total,)),
            pltpu.SemaphoreType.REGULAR((1 + len(STEPS),)),
        ],
        compiler_params=pltpu.CompilerParams(
            collective_id=0, has_side_effects=True, vmem_limit_bytes=60 * 1024 * 1024
        ),
        cost_estimate=pl.CostEstimate(flops=20_000_000, bytes_accessed=2_000_000, transcendentals=0),
    )(
        psi_block, occupied, entry_cell.reshape(table), entry_proj.reshape(table),
        entry_value.reshape(table), gains,
    )


def solution(mesh):
    in_specs = (
        P(None, "grid", None, None),
        P("band", "grid", None, None),
        P("grid"),
        P("grid"),
        P("grid"),
        P(),
    )
    out_specs = P(None, "grid", None, None)
    return jax.shard_map(
        per_device, mesh=mesh, in_specs=in_specs, out_specs=out_specs, check_vma=False
    )
```

```python
import functools

import jax
import jax.numpy as jnp
from jax import lax
from jax.experimental import pallas as pl
from jax.experimental.pallas import tpu as pltpu
from jax.sharding import PartitionSpec as P

screening = 0.5
mixing = 0.25
WIDTH = 3
LANES = 128
CORES = 2
XS, YS = 4, 4
STEPS = ((1, 2, 2), (2, 2, 1), (4, 3, 1))
YLO = 2
DIRECT = 2
GROUPS = 4
SHARE = 1
MESH = pl.DeviceIdType.MESH


def three_parts(x):
    first = x.astype(jnp.bfloat16)
    rest = x - first.astype(jnp.float32)
    second = rest.astype(jnp.bfloat16)
    third = (rest - second.astype(jnp.float32)).astype(jnp.bfloat16)
    return jnp.concatenate([first, second, third], axis=0)


def add_parts(x):
    n = x.shape[0] // 3
    return (x[:n] + x[n : 2 * n]) + x[2 * n :]


def as_row(x):
    return jnp.concatenate([x[i : i + 1] for i in range(x.shape[0])], axis=1)


def roll_sum(u):
    rows, lanes = u.shape[-2:]
    a = u.ndim - 2
    return (pltpu.roll(u, 1, a) + pltpu.roll(u, rows - 1, a)) + (
        pltpu.roll(u, 1, a + 1) + pltpu.roll(u, lanes - 1, a + 1)
    )


def kernel(
    nocc_cores,
    psi, occ, cell, proj, value, gain,
    out,
    psi_ext, occ_ext, cell_v, proj_v, value_v, gain_v,
    hot_lane, hot_proj, part, rs1, red1, rs2, kin, csum, cin, call_,
    local_sem, send_sem, recv_sem, step_sem,
):
    planes, rows = psi.shape[1], psi.shape[2]
    orbs = psi.shape[0] // CORES
    per = orbs // GROUPS
    ppx = planes // XS
    entries = cell.shape[0] * cell.shape[1]
    size = lax.axis_size("grid")
    ring = size // YLO
    g, n = lax.axis_index("grid"), lax.axis_index("band")
    c = lax.rem(n, CORES)
    y = lax.rem(lax.div(n, CORES), YS)
    x = lax.div(n, CORES * YS)

    def wrap(i, length):
        return jnp.where(i >= length, i - length, i)

    def band(xx, yy, cc):
        return (xx * YS + yy) * CORES + cc

    nxt, prv = (wrap(g + 1, size), n), (wrap(g + size - 1, size), n)
    sibling = (g, band(x, y, 1 - c))
    xpeers = [(g, band(wrap(x + m, XS), y, c)) for m in range(1, XS)]
    ypeers = [(g, band(x, wrap(y + m, YS), c)) for m in range(1, YS)]
    z = g
    for i in range(1, YLO):
        z = jnp.where(g >= i * ring, g - i * ring, z)
    turn = g - z

    def along(m, over=0):
        return (wrap(turn + wrap(z + m % ring, ring) + over * ring, size), n)

    partners = [nxt, prv]
    partners += [along(m, over) for over in range(1, YLO) for m in (-1, 1)]
    partners += [ypeers[i] for i in (0, -1) if ypeers]
    partners += [along(1), along(-1)] + [along(0, over) for over in range(1, YLO)]
    partners += [xpeers[i] for i in (0, -1) if xpeers] + [sibling]
    barrier = pltpu.get_barrier_semaphore()

    def signal(semaphore, device):
        pl.semaphore_signal(semaphore, inc=1, device_id=device, device_id_type=MESH)

    for device in partners:
        signal(barrier, device)

    def local(i, src, dst):
        copy = pltpu.make_async_copy(src, dst, local_sem.at[i])
        copy.start()
        return copy

    first = c * orbs
    load_entries = [
        local(0, cell, cell_v), local(1, proj, proj_v), local(2, value, value_v), local(3, gain, gain_v),
    ]
    load_psi = local(4, psi.at[pl.ds(first, orbs)], psi_ext.at[:, pl.ds(WIDTH, planes)])
    load_occ = local(5, occ.at[0], occ_ext.at[c, pl.ds(WIDTH, planes)])

    for copy in load_entries:
        copy.wait()
    cells, projs, values = as_row(cell_v[...]), as_row(proj_v[...]), as_row(value_v[...])
    cell_row, cell_lane = cells // LANES, cells % LANES
    proj_row, proj_lane = projs // LANES, projs % LANES
    lanes_at = lax.broadcasted_iota(jnp.int32, (LANES, entries), 0)
    hot_lane[...] = jnp.where(lanes_at == cell_lane, 1.0, 0.0).astype(jnp.bfloat16)
    hot_proj[...] = jnp.where(lanes_at == proj_lane, 1.0, 0.0).astype(jnp.bfloat16)
    eight = lax.broadcasted_iota(jnp.int32, (8, entries), 0)
    proj_mask = eight == proj_row

    load_psi.wait()
    load_occ.wait()
    nn = (((1,), (0,)), ((), ()))
    nt = (((1,), (1,)), ((), ()))

    def dot(a, b, dims):
        return lax.dot_general(a, b, dims, preferred_element_type=jnp.float32)

    cut = orbs // XS if orbs >= XS else 1
    for q in range(cut):
        own = psi_ext[x * cut + q, pl.ds(WIDTH, planes)].reshape(planes * rows, LANES)
        spread = add_parts(dot(three_parts(own), hot_lane[...], nn))
        at = lax.broadcasted_iota(jnp.int32, (planes * rows, entries), 0)
        picked = jnp.sum(jnp.where(at == cell_row, spread, 0.0), axis=0, keepdims=True)
        weight = jnp.where(proj_mask, picked * values, 0.0)
        csum[0, q] = add_parts(dot(three_parts(weight), hot_proj[...], nt))

    pl.semaphore_wait(barrier, len(partners))

    copies = []

    def send(src, dst, device):
        i = len(copies)
        copy = pltpu.make_async_remote_copy(
            src_ref=src, dst_ref=dst, send_sem=send_sem.at[i], recv_sem=recv_sem.at[i],
            device_id=device, device_id_type=MESH,
        )
        copy.start()
        copies.append(copy)
        return copy

    low, high = pl.ds(0, WIDTH), pl.ds(WIDTH + planes, WIDTH)
    upper, lower = pl.ds(planes, WIDTH), pl.ds(WIDTH, WIDTH)

    def halo(k):
        there = pl.ds(k * per, per)
        return [
            send(psi_ext.at[there, upper], psi_ext.at[there, low], nxt),
            send(psi_ext.at[there, lower], psi_ext.at[there, high], prv),
        ]

    word = [i for i, (_, terms, _) in enumerate(STEPS[:-1]) if terms == 2]
    bases = [sum(terms * over - 1 for _, terms, over in STEPS[:i]) for i in range(len(STEPS) + 1)]

    def far_first(peers, one):
        order = sorted(range(len(peers)), key=lambda m: -min(m + 1, len(peers) - m))
        sent = {m: one(m, peers[m]) for m in order}
        return [sent[m] for m in range(len(peers))]

    def coefficients(stage):
        distance, terms, over = STEPS[stage]
        if stage in word:
            signal(step_sem.at[1 + stage], along(distance))
        places = [0, -distance] if terms == 2 else [0, distance, -distance]
        devices = [along(m, o) for o in range(over) for m in places][1:]
        return [send(csum.at[stage], cin.at[bases[stage] + m], device) for m, device in enumerate(devices)]

    def collect(stage, sent):
        total = csum[stage]
        for m, copy in enumerate(sent):
            copy.wait_recv()
            total = total + cin[bases[stage] + m]
        csum[stage + 1] = total
        if stage in word:
            pl.semaphore_wait(step_sem.at[1 + stage], 1)

    stages = len(STEPS)
    steps = [coefficients(0)]

    def next_step():
        stage = len(steps) - 1
        if stage >= stages:
            return
        collect(stage, steps[stage])
        steps.append(coefficients(stage + 1) if stage + 1 < stages else None)

    occ_halo = [
        send(occ_ext.at[c, upper], occ_ext.at[c, low], nxt), send(occ_ext.at[c, lower], occ_ext.at[c, high], prv),
    ]
    centre = occ_ext.at[c, pl.ds(WIDTH, planes)]
    occ_core = send(centre, centre, sibling)
    halos = [halo(k) for k in range(GROUPS - 1)]
    greeted = [peers[-1] for peers in (xpeers, ypeers) if peers]
    for device in greeted:
        signal(step_sem.at[0], device)
    next_step()
    halos.append(halo(GROUPS - 1))
    for copy, part_ in zip(occ_halo, (low, high)):
        copy.wait_recv()
        block = occ_ext.at[c, part_]
        send(block, block, sibling)
    forwards = copies[-2:]

    a = 6.0 + screening

    def exchange(k):
        orbital = occ_ext[...]
        density = psi_ext[k][None] * orbital

        def shifted(m):
            return density[:, WIDTH + m : WIDTH + m + planes]

        d, once, twice, thrice = shifted(0), *(shifted(m) + shifted(-m) for m in range(1, WIDTH + 1))
        u = (a * d + 3.0 * once) + roll_sum(d)
        u = (((a * a + 6.0) * d + (2.0 * a) * once) + 3.0 * twice) + roll_sum(u)
        u = (((a**3 + 2.0 * a) * d + (a * a + 3.0) * once) + (a * twice + thrice)) + roll_sum(u)
        part[k] = jnp.sum(orbital[:, WIDTH : WIDTH + planes] * u, axis=0) * (1.0 / a**4)

    def scatter_x(k):
        def one(m, device):
            there = pl.ds(wrap(x + m + 1, XS) * ppx, ppx)
            return send(part.at[pl.ds(k * per, per), there], rs1.at[pl.ds(k * per, per), m], device)

        return far_first(xpeers, one)

    def sum_x(k, sent):
        own = pl.ds(k * per, per)
        total = part[own, pl.ds(x * ppx, ppx)]
        for m, copy in enumerate(sent):
            copy.wait_recv()
            total = total + rs1[own, m]
        red1[own] = total
        return far_first(ypeers, lambda m, device: send(red1.at[own], rs2.at[own, m], device))

    def share_coefficients():
        while len(steps) <= stages:
            next_step()
        gains = jnp.concatenate([gain_v[...], jnp.zeros((8 - gain_v.shape[0], LANES), jnp.float32)], axis=0)
        for q in range(cut):
            call_[x * cut + q] = csum[stages, q] * gains
        mine = pl.ds(x * cut, cut)
        return [send(call_.at[mine], call_.at[mine], device) for device in xpeers]

    first_sent, second_sent = [], []
    for k in range(GROUPS):
        for copy in halos[k]:
            copy.wait_recv()
        if k == 0:
            for copy in [occ_core] + forwards:
                copy.wait_recv()
            pl.semaphore_wait(step_sem.at[0], len(greeted))
        for i in range(k * per, (k + 1) * per):
            exchange(i)
        first_sent.append(scatter_x(k))
        if k == 0:
            next_step()
    for k in range(GROUPS):
        second_sent.append(sum_x(k, first_sent[k]))
        if k == SHARE:
            share = share_coefficients()

    for k in range(orbs):
        for q in range(ppx):
            at = WIDTH + x * ppx + q
            centre = psi_ext[k, at]
            around = (psi_ext[k, at + 1] + psi_ext[k, at - 1]) + roll_sum(centre)
            kin[k, q] = -0.5 * (around - 6.0 * centre)

    for copy in share:
        copy.wait_recv()
    found = add_parts(dot(three_parts(call_[...].reshape(orbs * 8, LANES)), hot_proj[...], nn))
    target = []
    for k in range(orbs):
        picked = jnp.sum(jnp.where(proj_mask, found[k * 8 : (k + 1) * 8], 0.0), axis=0, keepdims=True)
        target.append(picked * values)
    at = lax.broadcasted_iota(jnp.int32, (rows, entries), 0)
    for q in range(ppx):
        row_mask = at + (x * ppx + q) * rows == cell_row
        spread = jnp.concatenate([jnp.where(row_mask, t, 0.0) for t in target], axis=0)
        found = add_parts(dot(three_parts(spread), hot_lane[...], nt))
        for k in range(orbs):
            kin[k, q] = kin[k, q] + found[k * rows : (k + 1) * rows]

    xcross = [(g, band(wrap(x + m, XS), y, 1 - c)) for m in range(1, XS)]
    gathered = []
    for k in range(GROUPS):
        own = pl.ds(k * per, per)
        total = red1[own]
        for m, copy in enumerate(second_sent[k]):
            copy.wait_recv()
            total = total + rs2[own, m]
        there = pl.ds(first + k * per, per)
        block = out.at[there, pl.ds(x * ppx, ppx)]
        out[there, pl.ds(x * ppx, ppx)] = kin[own] - mixing * total
        last = k >= GROUPS - DIRECT
        sent = far_first(xpeers, lambda m, device: send(block, block, device))
        sent += far_first(xcross, lambda m, device: send(block, block, device)) if last else []
        gathered.append(sent + [send(block, block, sibling)])
    for k in range(GROUPS - DIRECT):
        for m, copy in enumerate(gathered[k][:-1]):
            copy.wait_recv()
            there = pl.ds(wrap(x + XS - 1 - m, XS) * ppx, ppx)
            block = out.at[pl.ds(first + k * per, per), there]
            gathered[k].append(send(block, block, sibling))
        gathered[k] = gathered[k][XS - 1 :]
    for sent in gathered:
        for copy in sent:
            copy.wait_recv()
    for copy in copies:
        copy.wait_send()


def n_copies():
    coefficient = sum(terms * over - 1 for _, terms, over in STEPS) + XS - 1
    return 3 + 2 + GROUPS * (2 + (XS - 1) + (YS - 1) + 2 * XS - 1) + coefficient


def per_device(psi_block, occupied, entry_cell, entry_proj, entry_value, proj_gain):
    nblock, planes, rows, lanes = psi_block.shape
    orbs = nblock // CORES
    entries = entry_cell.shape[0]
    f32 = jnp.float32
    table = (entries // LANES, LANES)
    ext = planes + 2 * WIDTH
    ppx = planes // XS
    cut = orbs // XS if orbs >= XS else 1
    gains = proj_gain.reshape(-1, LANES)
    total = n_copies()
    return pl.pallas_call(
        functools.partial(kernel, CORES),
        out_shape=pltpu.VMEM(psi_block.shape, f32),
        in_specs=[pl.BlockSpec(memory_space=pltpu.HBM)] * 6,
        out_specs=pl.BlockSpec(memory_space=pltpu.VMEM),
        scratch_shapes=[
            pltpu.VMEM((orbs, ext, rows, lanes), f32),
            pltpu.VMEM((CORES, ext, rows, lanes), f32),
            pltpu.VMEM(table, jnp.int32),
            pltpu.VMEM(table, jnp.int32),
            pltpu.VMEM(table, f32),
            pltpu.VMEM(gains.shape, f32),
            pltpu.VMEM((LANES, entries), jnp.bfloat16),
            pltpu.VMEM((LANES, entries), jnp.bfloat16),
            pltpu.VMEM((orbs, planes, rows, lanes), f32),
            pltpu.VMEM((orbs, XS - 1, ppx, rows, lanes), f32),
            pltpu.VMEM((orbs, ppx, rows, lanes), f32),
            pltpu.VMEM((orbs, YS - 1, ppx, rows, lanes), f32),
            pltpu.VMEM((orbs, ppx, rows, lanes), f32),
            pltpu.VMEM((len(STEPS) + 1, cut, 8, lanes), f32),
            pltpu.VMEM((sum(terms * over - 1 for _, terms, over in STEPS), cut, 8, lanes), f32),
            pltpu.VMEM((orbs, 8, lanes), f32),
            pltpu.SemaphoreType.DMA((6,)),
            pltpu.SemaphoreType.DMA((total,)),
            pltpu.SemaphoreType.DMA((total,)),
            pltpu.SemaphoreType.REGULAR((1 + len(STEPS),)),
        ],
        compiler_params=pltpu.CompilerParams(
            collective_id=0, has_side_effects=True, vmem_limit_bytes=60 * 1024 * 1024
        ),
        cost_estimate=pl.CostEstimate(flops=20_000_000, bytes_accessed=2_000_000, transcendentals=0),
    )(
        psi_block, occupied, entry_cell.reshape(table), entry_proj.reshape(table),
        entry_value.reshape(table), gains,
    )


def solution(mesh):
    in_specs = (
        P(None, "grid", None, None),
        P("band", "grid", None, None),
        P("grid"),
        P("grid"),
        P("grid"),
        P(),
    )
    out_specs = P(None, "grid", None, None)
    return jax.shard_map(
        per_device, mesh=mesh, in_specs=in_specs, out_specs=out_specs, check_vma=False
    )
```

```python
import functools

import jax
import jax.numpy as jnp
from jax import lax
from jax.experimental import pallas as pl
from jax.experimental.pallas import tpu as pltpu
from jax.sharding import PartitionSpec as P

screening = 0.5
mixing = 0.25
WIDTH = 3
LANES = 128
CORES = 2
XS, YS = 4, 4
STEPS = ((1, 2, 2), (2, 2, 1), (4, 3, 1))
YLO = 2
DIRECT = 2
GROUPS = 4
SHARE = 1
MESH = pl.DeviceIdType.MESH


def three_parts(x):
    first = x.astype(jnp.bfloat16)
    rest = x - first.astype(jnp.float32)
    second = rest.astype(jnp.bfloat16)
    third = (rest - second.astype(jnp.float32)).astype(jnp.bfloat16)
    return jnp.concatenate([first, second, third], axis=0)


def add_parts(x):
    n = x.shape[0] // 3
    return (x[:n] + x[n : 2 * n]) + x[2 * n :]


def as_row(x):
    return jnp.concatenate([x[i : i + 1] for i in range(x.shape[0])], axis=1)


def roll_sum(u):
    rows, lanes = u.shape[-2:]
    a = u.ndim - 2
    return (pltpu.roll(u, 1, a) + pltpu.roll(u, rows - 1, a)) + (
        pltpu.roll(u, 1, a + 1) + pltpu.roll(u, lanes - 1, a + 1)
    )


def kernel(
    nocc_cores,
    psi, occ, cell, proj, value, gain,
    out,
    psi_ext, occ_ext, cell_v, proj_v, value_v, gain_v,
    hot_lane, hot_proj, part, rs1, red1, rs2, kin, csum, cin, call_,
    local_sem, send_sem, recv_sem, step_sem,
):
    planes, rows = psi.shape[1], psi.shape[2]
    orbs = psi.shape[0] // CORES
    per = orbs // GROUPS
    ppx = planes // XS
    entries = cell.shape[0] * cell.shape[1]
    size = lax.axis_size("grid")
    ring = size // YLO
    g, n = lax.axis_index("grid"), lax.axis_index("band")
    c = lax.rem(n, CORES)
    y = lax.rem(lax.div(n, CORES), YS)
    x = lax.div(n, CORES * YS)

    def wrap(i, length):
        return jnp.where(i >= length, i - length, i)

    def band(xx, yy, cc):
        return (xx * YS + yy) * CORES + cc

    nxt, prv = (wrap(g + 1, size), n), (wrap(g + size - 1, size), n)
    sibling = (g, band(x, y, 1 - c))
    xpeers = [(g, band(wrap(x + m, XS), y, c)) for m in range(1, XS)]
    ypeers = [(g, band(x, wrap(y + m, YS), c)) for m in range(1, YS)]
    z = g
    for i in range(1, YLO):
        z = jnp.where(g >= i * ring, g - i * ring, z)
    turn = g - z

    def along(m, over=0):
        return (wrap(turn + wrap(z + m % ring, ring) + over * ring, size), n)

    partners = [nxt, prv]
    partners += [along(m, over) for over in range(1, YLO) for m in (-1, 1)]
    partners += [ypeers[i] for i in (0, -1) if ypeers]
    partners += [along(1), along(-1)] + [along(0, over) for over in range(1, YLO)]
    partners += [xpeers[i] for i in (0, -1) if xpeers] + [sibling]
    barrier = pltpu.get_barrier_semaphore()

    def signal(semaphore, device):
        pl.semaphore_signal(semaphore, inc=1, device_id=device, device_id_type=MESH)

    for device in partners:
        signal(barrier, device)

    def local(i, src, dst):
        copy = pltpu.make_async_copy(src, dst, local_sem.at[i])
        copy.start()
        return copy

    first = c * orbs
    load_entries = [
        local(0, cell, cell_v), local(1, proj, proj_v), local(2, value, value_v), local(3, gain, gain_v),
    ]
    load_psi = local(4, psi.at[pl.ds(first, orbs)], psi_ext.at[:, pl.ds(WIDTH, planes)])
    load_occ = local(5, occ.at[0], occ_ext.at[c, pl.ds(WIDTH, planes)])

    for copy in load_entries:
        copy.wait()
    cells, projs, values = as_row(cell_v[...]), as_row(proj_v[...]), as_row(value_v[...])
    cell_row, cell_lane = cells // LANES, cells % LANES
    proj_row, proj_lane = projs // LANES, projs % LANES
    lanes_at = lax.broadcasted_iota(jnp.int32, (LANES, entries), 0)
    hot_lane[...] = jnp.where(lanes_at == cell_lane, 1.0, 0.0).astype(jnp.bfloat16)
    hot_proj[...] = jnp.where(lanes_at == proj_lane, 1.0, 0.0).astype(jnp.bfloat16)
    eight = lax.broadcasted_iota(jnp.int32, (8, entries), 0)
    proj_mask = eight == proj_row

    load_psi.wait()
    load_occ.wait()
    nn = (((1,), (0,)), ((), ()))
    nt = (((1,), (1,)), ((), ()))

    def dot(a, b, dims):
        return lax.dot_general(a, b, dims, preferred_element_type=jnp.float32)

    cut = orbs // XS if orbs >= XS else 1
    for q in range(cut):
        own = psi_ext[x * cut + q, pl.ds(WIDTH, planes)].reshape(planes * rows, LANES)
        spread = add_parts(dot(three_parts(own), hot_lane[...], nn))
        at = lax.broadcasted_iota(jnp.int32, (planes * rows, entries), 0)
        picked = jnp.sum(jnp.where(at == cell_row, spread, 0.0), axis=0, keepdims=True)
        weight = jnp.where(proj_mask, picked * values, 0.0)
        csum[0, q] = add_parts(dot(three_parts(weight), hot_proj[...], nt))

    pl.semaphore_wait(barrier, len(partners))

    copies = []

    def send(src, dst, device):
        i = len(copies)
        copy = pltpu.make_async_remote_copy(
            src_ref=src, dst_ref=dst, send_sem=send_sem.at[i], recv_sem=recv_sem.at[i],
            device_id=device, device_id_type=MESH,
        )
        copy.start()
        copies.append(copy)
        return copy

    low, high = pl.ds(0, WIDTH), pl.ds(WIDTH + planes, WIDTH)
    upper, lower = pl.ds(planes, WIDTH), pl.ds(WIDTH, WIDTH)

    def halo(k):
        there = pl.ds(k * per, per)
        return [
            send(psi_ext.at[there, upper], psi_ext.at[there, low], nxt),
            send(psi_ext.at[there, lower], psi_ext.at[there, high], prv),
        ]

    word = [i for i, (_, terms, _) in enumerate(STEPS[:-1]) if terms == 2]
    bases = [sum(terms * over - 1 for _, terms, over in STEPS[:i]) for i in range(len(STEPS) + 1)]

    def far_first(peers, one):
        order = sorted(range(len(peers)), key=lambda m: -min(m + 1, len(peers) - m))
        sent = {m: one(m, peers[m]) for m in order}
        return [sent[m] for m in range(len(peers))]

    def coefficients(stage):
        distance, terms, over = STEPS[stage]
        if stage in word:
            signal(step_sem.at[1 + stage], along(distance))
        places = [0, -distance] if terms == 2 else [0, distance, -distance]
        devices = [along(m, o) for o in range(over) for m in places][1:]
        return [send(csum.at[stage], cin.at[bases[stage] + m], device) for m, device in enumerate(devices)]

    def collect(stage, sent):
        total = csum[stage]
        for m, copy in enumerate(sent):
            copy.wait_recv()
            total = total + cin[bases[stage] + m]
        csum[stage + 1] = total
        if stage in word:
            pl.semaphore_wait(step_sem.at[1 + stage], 1)

    stages = len(STEPS)
    steps = [coefficients(0)]

    def next_step():
        stage = len(steps) - 1
        if stage >= stages:
            return
        collect(stage, steps[stage])
        steps.append(coefficients(stage + 1) if stage + 1 < stages else None)

    occ_halo = [
        send(occ_ext.at[c, upper], occ_ext.at[c, low], nxt), send(occ_ext.at[c, lower], occ_ext.at[c, high], prv),
    ]
    centre = occ_ext.at[c, pl.ds(WIDTH, planes)]
    halos = [halo(0)]
    occ_core = send(centre, centre, sibling)
    halos += [halo(k) for k in range(1, GROUPS - 1)]
    greeted = [peers[-1] for peers in (xpeers, ypeers) if peers]
    for device in greeted:
        signal(step_sem.at[0], device)
    next_step()
    halos.append(halo(GROUPS - 1))
    for copy, part_ in zip(occ_halo, (low, high)):
        copy.wait_recv()
        block = occ_ext.at[c, part_]
        send(block, block, sibling)
    forwards = copies[-2:]

    a = 6.0 + screening

    def exchange(k):
        orbital = occ_ext[...]
        density = psi_ext[k][None] * orbital

        def shifted(m):
            return density[:, WIDTH + m : WIDTH + m + planes]

        d, once, twice, thrice = shifted(0), *(shifted(m) + shifted(-m) for m in range(1, WIDTH + 1))
        u = (a * d + 3.0 * once) + roll_sum(d)
        u = (((a * a + 6.0) * d + (2.0 * a) * once) + 3.0 * twice) + roll_sum(u)
        u = (((a**3 + 2.0 * a) * d + (a * a + 3.0) * once) + (a * twice + thrice)) + roll_sum(u)
        part[k] = jnp.sum(orbital[:, WIDTH : WIDTH + planes] * u, axis=0) * (1.0 / a**4)

    def scatter_x(k):
        def one(m, device):
            there = pl.ds(wrap(x + m + 1, XS) * ppx, ppx)
            return send(part.at[pl.ds(k * per, per), there], rs1.at[pl.ds(k * per, per), m], device)

        return far_first(xpeers, one)

    def sum_x(k, sent):
        own = pl.ds(k * per, per)
        total = part[own, pl.ds(x * ppx, ppx)]
        for m, copy in enumerate(sent):
            copy.wait_recv()
            total = total + rs1[own, m]
        red1[own] = total
        return far_first(ypeers, lambda m, device: send(red1.at[own], rs2.at[own, m], device))

    def share_coefficients():
        while len(steps) <= stages:
            next_step()
        gains = jnp.concatenate([gain_v[...], jnp.zeros((8 - gain_v.shape[0], LANES), jnp.float32)], axis=0)
        for q in range(cut):
            call_[x * cut + q] = csum[stages, q] * gains
        mine = pl.ds(x * cut, cut)
        return [send(call_.at[mine], call_.at[mine], device) for device in xpeers]

    first_sent, second_sent = [], []
    for k in range(GROUPS):
        for copy in halos[k]:
            copy.wait_recv()
        if k == 0:
            for copy in [occ_core] + forwards:
                copy.wait_recv()
            pl.semaphore_wait(step_sem.at[0], len(greeted))
        for i in range(k * per, (k + 1) * per):
            exchange(i)
        first_sent.append(scatter_x(k))
        if k == 0:
            next_step()
    for k in range(GROUPS):
        second_sent.append(sum_x(k, first_sent[k]))
        if k == SHARE:
            share = share_coefficients()

    for k in range(orbs):
        for q in range(ppx):
            at = WIDTH + x * ppx + q
            centre = psi_ext[k, at]
            around = (psi_ext[k, at + 1] + psi_ext[k, at - 1]) + roll_sum(centre)
            kin[k, q] = -0.5 * (around - 6.0 * centre)

    for copy in share:
        copy.wait_recv()
    found = add_parts(dot(three_parts(call_[...].reshape(orbs * 8, LANES)), hot_proj[...], nn))
    target = []
    for k in range(orbs):
        picked = jnp.sum(jnp.where(proj_mask, found[k * 8 : (k + 1) * 8], 0.0), axis=0, keepdims=True)
        target.append(picked * values)
    at = lax.broadcasted_iota(jnp.int32, (rows, entries), 0)
    for q in range(ppx):
        row_mask = at + (x * ppx + q) * rows == cell_row
        spread = jnp.concatenate([jnp.where(row_mask, t, 0.0) for t in target], axis=0)
        found = add_parts(dot(three_parts(spread), hot_lane[...], nt))
        for k in range(orbs):
            kin[k, q] = kin[k, q] + found[k * rows : (k + 1) * rows]

    xcross = [(g, band(wrap(x + m, XS), y, 1 - c)) for m in range(1, XS)]
    gathered = []
    for k in range(GROUPS):
        own = pl.ds(k * per, per)
        total = red1[own]
        for m, copy in enumerate(second_sent[k]):
            copy.wait_recv()
            total = total + rs2[own, m]
        there = pl.ds(first + k * per, per)
        block = out.at[there, pl.ds(x * ppx, ppx)]
        out[there, pl.ds(x * ppx, ppx)] = kin[own] - mixing * total
        last = k >= GROUPS - DIRECT
        sent = far_first(xpeers, lambda m, device: send(block, block, device))
        sent += far_first(xcross, lambda m, device: send(block, block, device)) if last else []
        gathered.append(sent + [send(block, block, sibling)])
    for k in range(GROUPS - DIRECT):
        for m, copy in enumerate(gathered[k][:-1]):
            copy.wait_recv()
            there = pl.ds(wrap(x + XS - 1 - m, XS) * ppx, ppx)
            block = out.at[pl.ds(first + k * per, per), there]
            gathered[k].append(send(block, block, sibling))
        gathered[k] = gathered[k][XS - 1 :]
    for sent in gathered:
        for copy in sent:
            copy.wait_recv()
    for copy in copies:
        copy.wait_send()


def n_copies():
    coefficient = sum(terms * over - 1 for _, terms, over in STEPS) + XS - 1
    return 3 + 2 + GROUPS * (2 + (XS - 1) + (YS - 1) + 2 * XS - 1) + coefficient


def per_device(psi_block, occupied, entry_cell, entry_proj, entry_value, proj_gain):
    nblock, planes, rows, lanes = psi_block.shape
    orbs = nblock // CORES
    entries = entry_cell.shape[0]
    f32 = jnp.float32
    table = (entries // LANES, LANES)
    ext = planes + 2 * WIDTH
    ppx = planes // XS
    cut = orbs // XS if orbs >= XS else 1
    gains = proj_gain.reshape(-1, LANES)
    total = n_copies()
    return pl.pallas_call(
        functools.partial(kernel, CORES),
        out_shape=pltpu.VMEM(psi_block.shape, f32),
        in_specs=[pl.BlockSpec(memory_space=pltpu.HBM)] * 6,
        out_specs=pl.BlockSpec(memory_space=pltpu.VMEM),
        scratch_shapes=[
            pltpu.VMEM((orbs, ext, rows, lanes), f32),
            pltpu.VMEM((CORES, ext, rows, lanes), f32),
            pltpu.VMEM(table, jnp.int32),
            pltpu.VMEM(table, jnp.int32),
            pltpu.VMEM(table, f32),
            pltpu.VMEM(gains.shape, f32),
            pltpu.VMEM((LANES, entries), jnp.bfloat16),
            pltpu.VMEM((LANES, entries), jnp.bfloat16),
            pltpu.VMEM((orbs, planes, rows, lanes), f32),
            pltpu.VMEM((orbs, XS - 1, ppx, rows, lanes), f32),
            pltpu.VMEM((orbs, ppx, rows, lanes), f32),
            pltpu.VMEM((orbs, YS - 1, ppx, rows, lanes), f32),
            pltpu.VMEM((orbs, ppx, rows, lanes), f32),
            pltpu.VMEM((len(STEPS) + 1, cut, 8, lanes), f32),
            pltpu.VMEM((sum(terms * over - 1 for _, terms, over in STEPS), cut, 8, lanes), f32),
            pltpu.VMEM((orbs, 8, lanes), f32),
            pltpu.SemaphoreType.DMA((6,)),
            pltpu.SemaphoreType.DMA((total,)),
            pltpu.SemaphoreType.DMA((total,)),
            pltpu.SemaphoreType.REGULAR((1 + len(STEPS),)),
        ],
        compiler_params=pltpu.CompilerParams(
            collective_id=0, has_side_effects=True, vmem_limit_bytes=60 * 1024 * 1024
        ),
        cost_estimate=pl.CostEstimate(flops=20_000_000, bytes_accessed=2_000_000, transcendentals=0),
    )(
        psi_block, occupied, entry_cell.reshape(table), entry_proj.reshape(table),
        entry_value.reshape(table), gains,
    )


def solution(mesh):
    in_specs = (
        P(None, "grid", None, None),
        P("band", "grid", None, None),
        P("grid"),
        P("grid"),
        P("grid"),
        P(),
    )
    out_specs = P(None, "grid", None, None)
    return jax.shard_map(
        per_device, mesh=mesh, in_specs=in_specs, out_specs=out_specs, check_vma=False
    )
```

```python
import functools

import jax
import jax.numpy as jnp
from jax import lax
from jax.experimental import pallas as pl
from jax.experimental.pallas import tpu as pltpu
from jax.sharding import PartitionSpec as P

screening = 0.5
mixing = 0.25
WIDTH = 3
LANES = 128
CORES = 2
XS, YS = 4, 4
STEPS = ((1, 2, 2), (2, 2, 1), (4, 3, 1))
YLO = 2
DIRECT = (2, 3)
GROUPS = 4
SHARE = 2
MESH = pl.DeviceIdType.MESH


def three_parts(x):
    first = x.astype(jnp.bfloat16)
    rest = x - first.astype(jnp.float32)
    second = rest.astype(jnp.bfloat16)
    third = (rest - second.astype(jnp.float32)).astype(jnp.bfloat16)
    return jnp.concatenate([first, second, third], axis=0)


def add_parts(x):
    n = x.shape[0] // 3
    return (x[:n] + x[n : 2 * n]) + x[2 * n :]


def as_row(x):
    return jnp.concatenate([x[i : i + 1] for i in range(x.shape[0])], axis=1)


def roll_sum(u):
    rows, lanes = u.shape[-2:]
    a = u.ndim - 2
    return (pltpu.roll(u, 1, a) + pltpu.roll(u, rows - 1, a)) + (
        pltpu.roll(u, 1, a + 1) + pltpu.roll(u, lanes - 1, a + 1)
    )


def kernel(
    nocc_cores,
    psi, occ, cell, proj, value, gain,
    out,
    psi_ext, occ_ext, cell_v, proj_v, value_v, gain_v,
    hot_lane, hot_proj, part, rs1, red1, rs2, kin, csum, cin, call_,
    local_sem, send_sem, recv_sem, step_sem,
):
    planes, rows = psi.shape[1], psi.shape[2]
    orbs = psi.shape[0] // CORES
    per = orbs // GROUPS
    ppx = planes // XS
    entries = cell.shape[0] * cell.shape[1]
    size = lax.axis_size("grid")
    ring = size // YLO
    g, n = lax.axis_index("grid"), lax.axis_index("band")
    c = lax.rem(n, CORES)
    y = lax.rem(lax.div(n, CORES), YS)
    x = lax.div(n, CORES * YS)

    def wrap(i, length):
        return jnp.where(i >= length, i - length, i)

    def band(xx, yy, cc):
        return (xx * YS + yy) * CORES + cc

    nxt, prv = (wrap(g + 1, size), n), (wrap(g + size - 1, size), n)
    sibling = (g, band(x, y, 1 - c))
    xpeers = [(g, band(wrap(x + m, XS), y, c)) for m in range(1, XS)]
    ypeers = [(g, band(x, wrap(y + m, YS), c)) for m in range(1, YS)]
    z = g
    for i in range(1, YLO):
        z = jnp.where(g >= i * ring, g - i * ring, z)
    turn = g - z

    def along(m, over=0):
        return (wrap(turn + wrap(z + m % ring, ring) + over * ring, size), n)

    partners = [nxt, prv]
    partners += [along(m, over) for over in range(1, YLO) for m in (-1, 1)]
    partners += [ypeers[i] for i in (0, -1) if ypeers]
    partners += [along(1), along(-1)] + [along(0, over) for over in range(1, YLO)]
    partners += [xpeers[i] for i in (0, -1) if xpeers] + [sibling]
    barrier = pltpu.get_barrier_semaphore()

    def signal(semaphore, device):
        pl.semaphore_signal(semaphore, inc=1, device_id=device, device_id_type=MESH)

    for device in partners:
        signal(barrier, device)

    def local(i, src, dst):
        copy = pltpu.make_async_copy(src, dst, local_sem.at[i])
        copy.start()
        return copy

    first = c * orbs
    load_entries = [
        local(0, cell, cell_v), local(1, proj, proj_v), local(2, value, value_v), local(3, gain, gain_v),
    ]
    load_psi = local(4, psi.at[pl.ds(first, orbs)], psi_ext.at[:, pl.ds(WIDTH, planes)])
    load_occ = local(5, occ.at[0], occ_ext.at[c, pl.ds(WIDTH, planes)])

    for copy in load_entries:
        copy.wait()
    cells, projs, values = as_row(cell_v[...]), as_row(proj_v[...]), as_row(value_v[...])
    cell_row, cell_lane = cells // LANES, cells % LANES
    proj_row, proj_lane = projs // LANES, projs % LANES
    lanes_at = lax.broadcasted_iota(jnp.int32, (LANES, entries), 0)
    hot_lane[...] = jnp.where(lanes_at == cell_lane, 1.0, 0.0).astype(jnp.bfloat16)
    hot_proj[...] = jnp.where(lanes_at == proj_lane, 1.0, 0.0).astype(jnp.bfloat16)
    eight = lax.broadcasted_iota(jnp.int32, (8, entries), 0)
    proj_mask = eight == proj_row

    load_psi.wait()
    load_occ.wait()
    nn = (((1,), (0,)), ((), ()))
    nt = (((1,), (1,)), ((), ()))

    def dot(a, b, dims):
        return lax.dot_general(a, b, dims, preferred_element_type=jnp.float32)

    cut = orbs // XS if orbs >= XS else 1
    for q in range(cut):
        own = psi_ext[x * cut + q, pl.ds(WIDTH, planes)].reshape(planes * rows, LANES)
        spread = add_parts(dot(three_parts(own), hot_lane[...], nn))
        at = lax.broadcasted_iota(jnp.int32, (planes * rows, entries), 0)
        picked = jnp.sum(jnp.where(at == cell_row, spread, 0.0), axis=0, keepdims=True)
        weight = jnp.where(proj_mask, picked * values, 0.0)
        csum[0, q] = add_parts(dot(three_parts(weight), hot_proj[...], nt))

    pl.semaphore_wait(barrier, len(partners))

    copies = []

    def send(src, dst, device):
        i = len(copies)
        copy = pltpu.make_async_remote_copy(
            src_ref=src, dst_ref=dst, send_sem=send_sem.at[i], recv_sem=recv_sem.at[i],
            device_id=device, device_id_type=MESH,
        )
        copy.start()
        copies.append(copy)
        return copy

    low, high = pl.ds(0, WIDTH), pl.ds(WIDTH + planes, WIDTH)
    upper, lower = pl.ds(planes, WIDTH), pl.ds(WIDTH, WIDTH)

    def halo(k):
        there = pl.ds(k * per, per)
        return [
            send(psi_ext.at[there, upper], psi_ext.at[there, low], nxt),
            send(psi_ext.at[there, lower], psi_ext.at[there, high], prv),
        ]

    word = [i for i, (_, terms, _) in enumerate(STEPS[:-1]) if terms == 2]
    bases = [sum(terms * over - 1 for _, terms, over in STEPS[:i]) for i in range(len(STEPS) + 1)]

    def far_first(peers, one):
        order = sorted(range(len(peers)), key=lambda m: -min(m + 1, len(peers) - m))
        sent = {m: one(m, peers[m]) for m in order}
        return [sent[m] for m in range(len(peers))]

    def coefficients(stage):
        distance, terms, over = STEPS[stage]
        if stage in word:
            signal(step_sem.at[1 + stage], along(distance))
        places = [0, -distance] if terms == 2 else [0, distance, -distance]
        devices = [along(m, o) for o in range(over) for m in places][1:]
        return [send(csum.at[stage], cin.at[bases[stage] + m], device) for m, device in enumerate(devices)]

    def collect(stage, sent):
        total = csum[stage]
        for m, copy in enumerate(sent):
            copy.wait_recv()
            total = total + cin[bases[stage] + m]
        csum[stage + 1] = total
        if stage in word:
            pl.semaphore_wait(step_sem.at[1 + stage], 1)

    stages = len(STEPS)
    steps = [coefficients(0)]

    def next_step():
        stage = len(steps) - 1
        if stage >= stages:
            return
        collect(stage, steps[stage])
        steps.append(coefficients(stage + 1) if stage + 1 < stages else None)

    occ_halo = [
        send(occ_ext.at[c, upper], occ_ext.at[c, low], nxt), send(occ_ext.at[c, lower], occ_ext.at[c, high], prv),
    ]
    centre = occ_ext.at[c, pl.ds(WIDTH, planes)]
    halos = [halo(0)]
    occ_core = send(centre, centre, sibling)
    halos += [halo(k) for k in range(1, GROUPS - 1)]
    greeted = [peers[-1] for peers in (xpeers, ypeers) if peers]
    for device in greeted:
        signal(step_sem.at[0], device)
    next_step()
    halos.append(halo(GROUPS - 1))
    for copy, part_ in zip(occ_halo, (low, high)):
        copy.wait_recv()
        block = occ_ext.at[c, part_]
        send(block, block, sibling)
    forwards = copies[-2:]

    a = 6.0 + screening

    def exchange(k):
        orbital = occ_ext[...]
        density = psi_ext[k][None] * orbital

        def shifted(m):
            return density[:, WIDTH + m : WIDTH + m + planes]

        d, once, twice, thrice = shifted(0), *(shifted(m) + shifted(-m) for m in range(1, WIDTH + 1))
        u = (a * d + 3.0 * once) + roll_sum(d)
        u = (((a * a + 6.0) * d + (2.0 * a) * once) + 3.0 * twice) + roll_sum(u)
        u = (((a**3 + 2.0 * a) * d + (a * a + 3.0) * once) + (a * twice + thrice)) + roll_sum(u)
        part[k] = jnp.sum(orbital[:, WIDTH : WIDTH + planes] * u, axis=0) * (1.0 / a**4)

    def scatter_x(k):
        def one(m, device):
            there = pl.ds(wrap(x + m + 1, XS) * ppx, ppx)
            return send(part.at[pl.ds(k * per, per), there], rs1.at[pl.ds(k * per, per), m], device)

        return far_first(xpeers, one)

    def sum_x(k, sent):
        own = pl.ds(k * per, per)
        total = part[own, pl.ds(x * ppx, ppx)]
        for m, copy in enumerate(sent):
            copy.wait_recv()
            total = total + rs1[own, m]
        red1[own] = total
        return far_first(ypeers, lambda m, device: send(red1.at[own], rs2.at[own, m], device))

    def share_coefficients():
        while len(steps) <= stages:
            next_step()
        gains = jnp.concatenate([gain_v[...], jnp.zeros((8 - gain_v.shape[0], LANES), jnp.float32)], axis=0)
        for q in range(cut):
            call_[x * cut + q] = csum[stages, q] * gains
        mine = pl.ds(x * cut, cut)
        return [send(call_.at[mine], call_.at[mine], device) for device in xpeers]

    first_sent, second_sent = [], []
    for k in range(GROUPS):
        for copy in halos[k]:
            copy.wait_recv()
        if k == 0:
            for copy in [occ_core] + forwards:
                copy.wait_recv()
            pl.semaphore_wait(step_sem.at[0], len(greeted))
        for i in range(k * per, (k + 1) * per):
            exchange(i)
        first_sent.append(scatter_x(k))
        if k == 0:
            next_step()
    for k in range(GROUPS):
        second_sent.append(sum_x(k, first_sent[k]))
        if k == SHARE:
            share = share_coefficients()

    for k in range(orbs):
        for q in range(ppx):
            at = WIDTH + x * ppx + q
            centre = psi_ext[k, at]
            around = (psi_ext[k, at + 1] + psi_ext[k, at - 1]) + roll_sum(centre)
            kin[k, q] = -0.5 * (around - 6.0 * centre)

    for copy in share:
        copy.wait_recv()
    found = add_parts(dot(three_parts(call_[...].reshape(orbs * 8, LANES)), hot_proj[...], nn))
    target = []
    for k in range(orbs):
        picked = jnp.sum(jnp.where(proj_mask, found[k * 8 : (k + 1) * 8], 0.0), axis=0, keepdims=True)
        target.append(picked * values)
    at = lax.broadcasted_iota(jnp.int32, (rows, entries), 0)
    for q in range(ppx):
        row_mask = at + (x * ppx + q) * rows == cell_row
        spread = jnp.concatenate([jnp.where(row_mask, t, 0.0) for t in target], axis=0)
        found = add_parts(dot(three_parts(spread), hot_lane[...], nt))
        for k in range(orbs):
            kin[k, q] = kin[k, q] + found[k * rows : (k + 1) * rows]

    xcross = [(g, band(wrap(x + m, XS), y, 1 - c)) for m in range(1, XS)]
    gathered = []
    for k in range(GROUPS):
        own = pl.ds(k * per, per)
        total = red1[own]
        for m, copy in enumerate(second_sent[k]):
            copy.wait_recv()
            total = total + rs2[own, m]
        there = pl.ds(first + k * per, per)
        block = out.at[there, pl.ds(x * ppx, ppx)]
        out[there, pl.ds(x * ppx, ppx)] = kin[own] - mixing * total
        last = k in DIRECT
        sent = far_first(xpeers, lambda m, device: send(block, block, device))
        sent += far_first(xcross, lambda m, device: send(block, block, device)) if last else []
        gathered.append(sent + [send(block, block, sibling)])
    for k in (k for k in range(GROUPS) if k not in DIRECT):
        for m, copy in enumerate(gathered[k][:-1]):
            copy.wait_recv()
            there = pl.ds(wrap(x + XS - 1 - m, XS) * ppx, ppx)
            block = out.at[pl.ds(first + k * per, per), there]
            gathered[k].append(send(block, block, sibling))
        gathered[k] = gathered[k][XS - 1 :]
    for sent in gathered:
        for copy in sent:
            copy.wait_recv()
    for copy in copies:
        copy.wait_send()


def n_copies():
    coefficient = sum(terms * over - 1 for _, terms, over in STEPS) + XS - 1
    return 3 + 2 + GROUPS * (2 + (XS - 1) + (YS - 1) + 2 * XS - 1) + coefficient


def per_device(psi_block, occupied, entry_cell, entry_proj, entry_value, proj_gain):
    nblock, planes, rows, lanes = psi_block.shape
    orbs = nblock // CORES
    entries = entry_cell.shape[0]
    f32 = jnp.float32
    table = (entries // LANES, LANES)
    ext = planes + 2 * WIDTH
    ppx = planes // XS
    cut = orbs // XS if orbs >= XS else 1
    gains = proj_gain.reshape(-1, LANES)
    total = n_copies()
    return pl.pallas_call(
        functools.partial(kernel, CORES),
        out_shape=pltpu.VMEM(psi_block.shape, f32),
        in_specs=[pl.BlockSpec(memory_space=pltpu.HBM)] * 6,
        out_specs=pl.BlockSpec(memory_space=pltpu.VMEM),
        scratch_shapes=[
            pltpu.VMEM((orbs, ext, rows, lanes), f32),
            pltpu.VMEM((CORES, ext, rows, lanes), f32),
            pltpu.VMEM(table, jnp.int32),
            pltpu.VMEM(table, jnp.int32),
            pltpu.VMEM(table, f32),
            pltpu.VMEM(gains.shape, f32),
            pltpu.VMEM((LANES, entries), jnp.bfloat16),
            pltpu.VMEM((LANES, entries), jnp.bfloat16),
            pltpu.VMEM((orbs, planes, rows, lanes), f32),
            pltpu.VMEM((orbs, XS - 1, ppx, rows, lanes), f32),
            pltpu.VMEM((orbs, ppx, rows, lanes), f32),
            pltpu.VMEM((orbs, YS - 1, ppx, rows, lanes), f32),
            pltpu.VMEM((orbs, ppx, rows, lanes), f32),
            pltpu.VMEM((len(STEPS) + 1, cut, 8, lanes), f32),
            pltpu.VMEM((sum(terms * over - 1 for _, terms, over in STEPS), cut, 8, lanes), f32),
            pltpu.VMEM((orbs, 8, lanes), f32),
            pltpu.SemaphoreType.DMA((6,)),
            pltpu.SemaphoreType.DMA((total,)),
            pltpu.SemaphoreType.DMA((total,)),
            pltpu.SemaphoreType.REGULAR((1 + len(STEPS),)),
        ],
        compiler_params=pltpu.CompilerParams(
            collective_id=0, has_side_effects=True, vmem_limit_bytes=60 * 1024 * 1024
        ),
        cost_estimate=pl.CostEstimate(flops=20_000_000, bytes_accessed=2_000_000, transcendentals=0),
    )(
        psi_block, occupied, entry_cell.reshape(table), entry_proj.reshape(table),
        entry_value.reshape(table), gains,
    )


def solution(mesh):
    in_specs = (
        P(None, "grid", None, None),
        P("band", "grid", None, None),
        P("grid"),
        P("grid"),
        P("grid"),
        P(),
    )
    out_specs = P(None, "grid", None, None)
    return jax.shard_map(
        per_device, mesh=mesh, in_specs=in_specs, out_specs=out_specs, check_vma=False
    )
```

```python
import functools

import jax
import jax.numpy as jnp
from jax import lax
from jax.experimental import pallas as pl
from jax.experimental.pallas import tpu as pltpu
from jax.sharding import PartitionSpec as P

screening = 0.5
mixing = 0.25
WIDTH = 3
LANES = 128
CORES = 2
XS, YS = 4, 4
STEPS = ((1, 2, 2), (2, 2, 1), (4, 3, 1))
YLO = 2
DIRECT = (2, 3)
GROUPS = 4
SHARE = 2
MESH = pl.DeviceIdType.MESH


def three_parts(x):
    first = x.astype(jnp.bfloat16)
    rest = x - first.astype(jnp.float32)
    second = rest.astype(jnp.bfloat16)
    third = (rest - second.astype(jnp.float32)).astype(jnp.bfloat16)
    return jnp.concatenate([first, second, third], axis=0)


def add_parts(x):
    n = x.shape[0] // 3
    return (x[:n] + x[n : 2 * n]) + x[2 * n :]


def as_row(x):
    return jnp.concatenate([x[i : i + 1] for i in range(x.shape[0])], axis=1)


def roll_sum(u):
    rows, lanes = u.shape[-2:]
    a = u.ndim - 2
    return (pltpu.roll(u, 1, a) + pltpu.roll(u, rows - 1, a)) + (
        pltpu.roll(u, 1, a + 1) + pltpu.roll(u, lanes - 1, a + 1)
    )


def kernel(
    nocc_cores,
    psi, occ, cell, proj, value, gain,
    out,
    psi_ext, occ_ext, cell_v, proj_v, value_v, gain_v,
    hot_lane, hot_proj, part, rs1, red1, rs2, kin, csum, cin, call_,
    local_sem, send_sem, recv_sem, step_sem,
):
    planes, rows = psi.shape[1], psi.shape[2]
    orbs = psi.shape[0] // CORES
    per = orbs // GROUPS
    ppx = planes // XS
    entries = cell.shape[0] * cell.shape[1]
    size = lax.axis_size("grid")
    ring = size // YLO
    g, n = lax.axis_index("grid"), lax.axis_index("band")
    c = lax.rem(n, CORES)
    y = lax.rem(lax.div(n, CORES), YS)
    x = lax.div(n, CORES * YS)

    def wrap(i, length):
        return jnp.where(i >= length, i - length, i)

    def band(xx, yy, cc):
        return (xx * YS + yy) * CORES + cc

    nxt, prv = (wrap(g + 1, size), n), (wrap(g + size - 1, size), n)
    sibling = (g, band(x, y, 1 - c))
    xpeers = [(g, band(wrap(x + m, XS), y, c)) for m in range(1, XS)]
    ypeers = [(g, band(x, wrap(y + m, YS), c)) for m in range(1, YS)]
    z = g
    for i in range(1, YLO):
        z = jnp.where(g >= i * ring, g - i * ring, z)
    turn = g - z

    def along(m, over=0):
        return (wrap(turn + wrap(z + m % ring, ring) + over * ring, size), n)

    partners = [nxt, prv]
    partners += [along(m, over) for over in range(1, YLO) for m in (-1, 1)]
    partners += [ypeers[i] for i in (0, -1) if ypeers]
    partners += [along(1), along(-1)] + [along(0, over) for over in range(1, YLO)]
    partners += [xpeers[i] for i in (0, -1) if xpeers] + [sibling]
    barrier = pltpu.get_barrier_semaphore()

    def signal(semaphore, device):
        pl.semaphore_signal(semaphore, inc=1, device_id=device, device_id_type=MESH)

    for device in partners:
        signal(barrier, device)

    def local(i, src, dst):
        copy = pltpu.make_async_copy(src, dst, local_sem.at[i])
        copy.start()
        return copy

    first = c * orbs
    load_entries = [
        local(0, cell, cell_v), local(1, proj, proj_v), local(2, value, value_v), local(3, gain, gain_v),
    ]
    load_psi = local(4, psi.at[pl.ds(first, orbs)], psi_ext.at[:, pl.ds(WIDTH, planes)])
    load_occ = local(5, occ.at[0], occ_ext.at[c, pl.ds(WIDTH, planes)])

    for copy in load_entries:
        copy.wait()
    cells, projs, values = as_row(cell_v[...]), as_row(proj_v[...]), as_row(value_v[...])
    cell_row, cell_lane = cells // LANES, cells % LANES
    proj_row, proj_lane = projs // LANES, projs % LANES
    lanes_at = lax.broadcasted_iota(jnp.int32, (LANES, entries), 0)
    hot_lane[...] = jnp.where(lanes_at == cell_lane, 1.0, 0.0).astype(jnp.bfloat16)
    hot_proj[...] = jnp.where(lanes_at == proj_lane, 1.0, 0.0).astype(jnp.bfloat16)
    eight = lax.broadcasted_iota(jnp.int32, (8, entries), 0)
    proj_mask = eight == proj_row

    load_psi.wait()
    load_occ.wait()
    nn = (((1,), (0,)), ((), ()))
    nt = (((1,), (1,)), ((), ()))

    def dot(a, b, dims):
        return lax.dot_general(a, b, dims, preferred_element_type=jnp.float32)

    cut = orbs // XS if orbs >= XS else 1
    for q in range(cut):
        own = psi_ext[x * cut + q, pl.ds(WIDTH, planes)].reshape(planes * rows, LANES)
        spread = add_parts(dot(three_parts(own), hot_lane[...], nn))
        at = lax.broadcasted_iota(jnp.int32, (planes * rows, entries), 0)
        picked = jnp.sum(jnp.where(at == cell_row, spread, 0.0), axis=0, keepdims=True)
        weight = jnp.where(proj_mask, picked * values, 0.0)
        csum[0, q] = add_parts(dot(three_parts(weight), hot_proj[...], nt))

    pl.semaphore_wait(barrier, len(partners))

    copies = []

    def send(src, dst, device):
        i = len(copies)
        copy = pltpu.make_async_remote_copy(
            src_ref=src, dst_ref=dst, send_sem=send_sem.at[i], recv_sem=recv_sem.at[i],
            device_id=device, device_id_type=MESH,
        )
        copy.start()
        copies.append(copy)
        return copy

    low, high = pl.ds(0, WIDTH), pl.ds(WIDTH + planes, WIDTH)
    upper, lower = pl.ds(planes, WIDTH), pl.ds(WIDTH, WIDTH)

    def halo(k):
        there = pl.ds(k * per, per)
        return [
            send(psi_ext.at[there, upper], psi_ext.at[there, low], nxt),
            send(psi_ext.at[there, lower], psi_ext.at[there, high], prv),
        ]

    word = [i for i, (_, terms, _) in enumerate(STEPS[:-1]) if terms == 2]
    bases = [sum(terms * over - 1 for _, terms, over in STEPS[:i]) for i in range(len(STEPS) + 1)]

    def far_first(peers, one):
        order = sorted(range(len(peers)), key=lambda m: -min(m + 1, len(peers) - m))
        sent = {m: one(m, peers[m]) for m in order}
        return [sent[m] for m in range(len(peers))]

    def coefficients(stage):
        distance, terms, over = STEPS[stage]
        if stage in word:
            signal(step_sem.at[1 + stage], along(distance))
        places = [0, -distance] if terms == 2 else [0, distance, -distance]
        devices = [along(m, o) for o in range(over) for m in places][1:]
        return [send(csum.at[stage], cin.at[bases[stage] + m], device) for m, device in enumerate(devices)]

    def collect(stage, sent):
        total = csum[stage]
        for m, copy in enumerate(sent):
            copy.wait_recv()
            total = total + cin[bases[stage] + m]
        csum[stage + 1] = total
        if stage in word:
            pl.semaphore_wait(step_sem.at[1 + stage], 1)

    stages = len(STEPS)
    steps = [coefficients(0)]

    def next_step():
        stage = len(steps) - 1
        if stage >= stages:
            return
        collect(stage, steps[stage])
        steps.append(coefficients(stage + 1) if stage + 1 < stages else None)

    occ_halo = [
        send(occ_ext.at[c, upper], occ_ext.at[c, low], nxt), send(occ_ext.at[c, lower], occ_ext.at[c, high], prv),
    ]
    centre = occ_ext.at[c, pl.ds(WIDTH, planes)]
    halos = [halo(0)]
    occ_core = send(centre, centre, sibling)
    halos += [halo(k) for k in range(1, GROUPS - 1)]
    greeted = [peers[-1] for peers in (xpeers, ypeers) if peers]
    for device in greeted:
        signal(step_sem.at[0], device)
    next_step()
    halos.append(halo(GROUPS - 1))
    for copy, part_ in zip(occ_halo, (low, high)):
        copy.wait_recv()
        block = occ_ext.at[c, part_]
        send(block, block, sibling)
    forwards = copies[-2:]

    a = 6.0 + screening

    def exchange(k):
        orbital = occ_ext[...]
        density = psi_ext[k][None] * orbital

        def shifted(m):
            return density[:, WIDTH + m : WIDTH + m + planes]

        d, once, twice, thrice = shifted(0), *(shifted(m) + shifted(-m) for m in range(1, WIDTH + 1))
        u = (a * d + 3.0 * once) + roll_sum(d)
        u = (((a * a + 6.0) * d + (2.0 * a) * once) + 3.0 * twice) + roll_sum(u)
        u = (((a**3 + 2.0 * a) * d + (a * a + 3.0) * once) + (a * twice + thrice)) + roll_sum(u)
        part[k] = jnp.sum(orbital[:, WIDTH : WIDTH + planes] * u, axis=0) * (1.0 / a**4)

    def scatter_x(k):
        def one(m, device):
            there = pl.ds(wrap(x + m + 1, XS) * ppx, ppx)
            return send(part.at[pl.ds(k * per, per), there], rs1.at[pl.ds(k * per, per), m], device)

        return far_first(xpeers, one)

    def sum_x(k, sent):
        own = pl.ds(k * per, per)
        total = part[own, pl.ds(x * ppx, ppx)]
        for m, copy in enumerate(sent):
            copy.wait_recv()
            total = total + rs1[own, m]
        red1[own] = total
        return far_first(ypeers, lambda m, device: send(red1.at[own], rs2.at[own, m], device))

    def share_coefficients():
        while len(steps) <= stages:
            next_step()
        gains = jnp.concatenate([gain_v[...], jnp.zeros((8 - gain_v.shape[0], LANES), jnp.float32)], axis=0)
        for q in range(cut):
            call_[x * cut + q] = csum[stages, q] * gains
        mine = pl.ds(x * cut, cut)
        return [send(call_.at[mine], call_.at[mine], device) for device in xpeers]

    first_sent, second_sent = [], []
    for k in range(GROUPS):
        for copy in halos[k]:
            copy.wait_recv()
        if k == 0:
            for copy in [occ_core] + forwards:
                copy.wait_recv()
            pl.semaphore_wait(step_sem.at[0], len(greeted))
        for i in range(k * per, (k + 1) * per):
            exchange(i)
        first_sent.append(scatter_x(k))
        if k == 0:
            next_step()
    for k in range(GROUPS):
        second_sent.append(sum_x(k, first_sent[k]))
        if k == SHARE:
            share = share_coefficients()

    for k in range(orbs):
        for q in range(ppx):
            at = WIDTH + x * ppx + q
            centre = psi_ext[k, at]
            around = (psi_ext[k, at + 1] + psi_ext[k, at - 1]) + roll_sum(centre)
            kin[k, q] = -0.5 * (around - 6.0 * centre)

    for copy in share:
        copy.wait_recv()
    found = add_parts(dot(three_parts(call_[...].reshape(orbs * 8, LANES)), hot_proj[...], nn))
    target = []
    for k in range(orbs):
        picked = jnp.sum(jnp.where(proj_mask, found[k * 8 : (k + 1) * 8], 0.0), axis=0, keepdims=True)
        target.append(picked * values)
    at = lax.broadcasted_iota(jnp.int32, (rows, entries), 0)
    for q in range(ppx):
        row_mask = at + (x * ppx + q) * rows == cell_row
        spread = jnp.concatenate([jnp.where(row_mask, t, 0.0) for t in target], axis=0)
        found = add_parts(dot(three_parts(spread), hot_lane[...], nt))
        for k in range(orbs):
            kin[k, q] = kin[k, q] + found[k * rows : (k + 1) * rows]

    xcross = [(g, band(wrap(x + m, XS), y, 1 - c)) for m in range(1, XS)]
    gathered = []
    for k in range(GROUPS):
        own = pl.ds(k * per, per)
        total = red1[own]
        for m, copy in enumerate(second_sent[k]):
            copy.wait_recv()
            total = total + rs2[own, m]
        there = pl.ds(first + k * per, per)
        block = out.at[there, pl.ds(x * ppx, ppx)]
        out[there, pl.ds(x * ppx, ppx)] = kin[own] - mixing * total
        last = k in DIRECT
        sent = far_first(xpeers, lambda m, device: send(block, block, device))
        sent += far_first(xcross, lambda m, device: send(block, block, device)) if last else []
        gathered.append(sent + [send(block, block, sibling)])
    early = [k for k in range(GROUPS) if k not in DIRECT]
    for m in range(XS - 1):
        for k in early:
            gathered[k][m].wait_recv()
        there = pl.ds(wrap(x + XS - 1 - m, XS) * ppx, ppx)
        block = out.at[pl.ds(first, len(early) * per), there]
        gathered[0].append(send(block, block, sibling))
    for k in early:
        gathered[k] = gathered[k][XS - 1 :]
    for sent in gathered:
        for copy in sent:
            copy.wait_recv()
    for copy in copies:
        copy.wait_send()


def n_copies():
    coefficient = sum(terms * over - 1 for _, terms, over in STEPS) + XS - 1
    return 3 + 2 + GROUPS * (2 + (XS - 1) + (YS - 1) + 2 * XS - 1) + coefficient


def per_device(psi_block, occupied, entry_cell, entry_proj, entry_value, proj_gain):
    nblock, planes, rows, lanes = psi_block.shape
    orbs = nblock // CORES
    entries = entry_cell.shape[0]
    f32 = jnp.float32
    table = (entries // LANES, LANES)
    ext = planes + 2 * WIDTH
    ppx = planes // XS
    cut = orbs // XS if orbs >= XS else 1
    gains = proj_gain.reshape(-1, LANES)
    total = n_copies()
    return pl.pallas_call(
        functools.partial(kernel, CORES),
        out_shape=pltpu.VMEM(psi_block.shape, f32),
        in_specs=[pl.BlockSpec(memory_space=pltpu.HBM)] * 6,
        out_specs=pl.BlockSpec(memory_space=pltpu.VMEM),
        scratch_shapes=[
            pltpu.VMEM((orbs, ext, rows, lanes), f32),
            pltpu.VMEM((CORES, ext, rows, lanes), f32),
            pltpu.VMEM(table, jnp.int32),
            pltpu.VMEM(table, jnp.int32),
            pltpu.VMEM(table, f32),
            pltpu.VMEM(gains.shape, f32),
            pltpu.VMEM((LANES, entries), jnp.bfloat16),
            pltpu.VMEM((LANES, entries), jnp.bfloat16),
            pltpu.VMEM((orbs, planes, rows, lanes), f32),
            pltpu.VMEM((orbs, XS - 1, ppx, rows, lanes), f32),
            pltpu.VMEM((orbs, ppx, rows, lanes), f32),
            pltpu.VMEM((orbs, YS - 1, ppx, rows, lanes), f32),
            pltpu.VMEM((orbs, ppx, rows, lanes), f32),
            pltpu.VMEM((len(STEPS) + 1, cut, 8, lanes), f32),
            pltpu.VMEM((sum(terms * over - 1 for _, terms, over in STEPS), cut, 8, lanes), f32),
            pltpu.VMEM((orbs, 8, lanes), f32),
            pltpu.SemaphoreType.DMA((6,)),
            pltpu.SemaphoreType.DMA((total,)),
            pltpu.SemaphoreType.DMA((total,)),
            pltpu.SemaphoreType.REGULAR((1 + len(STEPS),)),
        ],
        compiler_params=pltpu.CompilerParams(
            collective_id=0, has_side_effects=True, vmem_limit_bytes=60 * 1024 * 1024
        ),
        cost_estimate=pl.CostEstimate(flops=20_000_000, bytes_accessed=2_000_000, transcendentals=0),
    )(
        psi_block, occupied, entry_cell.reshape(table), entry_proj.reshape(table),
        entry_value.reshape(table), gains,
    )


def solution(mesh):
    in_specs = (
        P(None, "grid", None, None),
        P("band", "grid", None, None),
        P("grid"),
        P("grid"),
        P("grid"),
        P(),
    )
    out_specs = P(None, "grid", None, None)
    return jax.shard_map(
        per_device, mesh=mesh, in_specs=in_specs, out_specs=out_specs, check_vma=False
    )
```
